256 devices in a mesh: dp: 8 (over z), expert: 32 (over y, x, core).
Axes of the slice: x: 4, y: 4, z: 8, core: 2. Of those that a mesh axis runs over, the one named last changes fastest.
Arguments:
- tokens: bfloat16 [32768, 4096], P(('dp', 'expert')), may hold values from -6 to 6
- cotangent: bfloat16 [32768, 4096], P(('dp', 'expert')), may hold values from -6 to 6
- expert_ids: int32 [32768, 2], P(('dp', 'expert')), may hold values from 0 to 15, all different within a row; in each aligned block of 128 rows (0 to 127, 128 to 255, ...) at most 18 rows name the same one
- probs: float32 [32768, 2], P(('dp', 'expert')), may hold values from 0.1 to 1
- w_gate: bfloat16 [32, 4096, 384], P('expert'), may hold values from -0.09375 to 0.09375
- w_up: bfloat16 [32, 4096, 384], P('expert'), may hold values from -0.09375 to 0.09375
- w_down: bfloat16 [32, 384, 4096], P('expert'), may hold values from -0.21875 to 0.21875
Outputs:
- grad_tokens: bfloat16 [32768, 4096], P(('dp', 'expert'))
- grad_gate: bfloat16 [32, 4096, 384], P('expert', 'dp')
- grad_up: bfloat16 [32, 4096, 384], P('expert', 'dp')
- grad_down: bfloat16 [32, 384, 4096], P('expert', None, 'dp')
The draws below stay inside these ranges and needn't reach their ends.
Inputs may be any that keep to these rules, and one draw needn't show every extreme that they name: `expert_ids`: each row names 2 different experts; within each device block of 128 rows no expert is named by more than 18 rows, a bound that some block reaches.
All inputs are finite; a program needn't handle non-finite values.
Results may differ from the reference program's by a relative error of at most 0.019.
Values may be sent and summed in bfloat16 or wider, within the bound.
A program may use at most 128 MiB of HBM per device.

```python
import math
import jax
import jax.numpy as jnp
import numpy as np
from jax import lax

D = 4096
FF = 768
SPLIT = 2
TOPK = 2
TOK_DEV = 128
FDEV = 384
EXPERTS = 16
CAP = 18
TOKENS = 32768
N_DP = 8
N_EXPERT = 32


def steps_of(stream_key, dims, split, least, top_value):
    def one(axis_at, parts):
        draws = jax.random.uniform(jax.random.fold_in(jax.random.fold_in(stream_key, 6), axis_at), (parts,), jnp.float32, least / len(split), top_value / len(split))
        return jnp.repeat(jnp.exp(draws), dims[axis_at] // parts).reshape((-1,) + (1,) * (len(dims) - axis_at - 1))

    loudness = one(*split[0])
    for cut in split[1:]:
        loudness = loudness * one(*cut)
    return loudness


def shared_out(stream_key, own, number, rows, amount, top, limit, slope):
    sequence = jax.random.permutation(stream_key, amount)
    packed, usual = portions_of(amount, rows * top, limit, slope, True), portions_of(amount, rows * top, limit, slope, False)
    places = jnp.arange(amount)

    def named(sizes, offset_by):
        used = int((sizes > 0).sum())
        fixed = max(1, used // 4)
        shifted = fixed + (places - fixed + offset_by * (used - fixed)) % max(1, amount - fixed)
        return jnp.zeros((amount,), jnp.int32).at[sequence[jnp.where(places < fixed, places, shifted)]].set(jnp.asarray(sizes, jnp.int32))

    sizes = jnp.where(number % 4 == 0, named(packed, number // 4), named(usual, number - number // 4 - 1))
    mixed = jax.random.permutation(jax.random.fold_in(own, 3), amount)
    donor, receiver = mixed[0:amount // 2 * 2:2], mixed[1:amount // 2 * 2:2]
    slack = jnp.minimum(sizes[donor] - 1, limit - sizes[receiver]) // 2
    slack = jnp.where((donor == sequence[0]) | (receiver == sequence[0]) | (sizes[receiver] == 0), 0, jnp.maximum(slack, 0))
    shifted = jax.random.randint(jax.random.fold_in(own, 4), (amount // 2,), 0, 1 << 20) % (slack + 1)
    sizes = sizes.at[donor].add(-shifted).at[receiver].add(shifted)
    items = jnp.searchsorted(jnp.cumsum(sizes), jnp.arange(rows * top), side="right").astype(jnp.int32)
    table = items.reshape(top, rows).T
    table = table[jax.random.permutation(jax.random.fold_in(own, 1), rows)]
    offset_by = jax.random.randint(jax.random.fold_in(own, 2), (rows, 1), 0, top)
    return jnp.take_along_axis(table, (jnp.arange(top)[None, :] + offset_by) % top, axis=1)


def portions_of(number_of, total, bound, slope, full):
    loads = [(1 << 20) // math.isqrt(standing ** slope) + 1 for standing in range(1, number_of + 1)]
    largest = bound if full else min(bound, max(-(-total // number_of), total * loads[0] // sum(loads)))
    least = 1 if total - largest >= number_of - 1 else 0
    holding, rest = [largest] + [least] * (number_of - 1), total - largest - least * (number_of - 1)
    while rest > 0:
        free = [i for i in range(1, number_of) if holding[i] < largest] or [i for i in range(1, number_of) if holding[i] < bound]
        whole, left = sum([loads[i] for i in free]), rest
        for i in free:
            extra = min(bound - holding[i], max(1, left * loads[i] // whole), rest)
            holding[i] = holding[i] + extra
            rest = rest - extra
    return np.array(holding)


def bell_draw(rng, shape, deviation, bound, shards=(), kind=jnp.bfloat16):
    values = deviation * jax.random.normal(rng, shape, jnp.float32)
    if shards:
        values = values * steps_of(rng, shape, shards, -0.22, 0.18)
    return jnp.clip(values, -bound, bound).astype(kind)


def setup_inputs(seed: int = 0) -> dict:
    key_of = jax.random.split(jax.random.key(seed), 8)
    tokens = bell_draw(key_of[0], (TOKENS, D), 1.0, 6.0, ((0, 256),))
    cotangent = bell_draw(key_of[1], (TOKENS, D), 1.0, 6.0, ((0, 256),))
    expert_ids_keys = jax.random.split(jax.random.fold_in(key_of[2], 1), TOKENS // TOK_DEV)
    expert_ids_turns = jax.random.permutation(jax.random.fold_in(key_of[2], 3), TOKENS // TOK_DEV)
    expert_ids = jax.vmap(lambda own, number: shared_out(jax.random.fold_in(key_of[2], 2), own, number, TOK_DEV, EXPERTS, TOPK, CAP, 2))(expert_ids_keys, expert_ids_turns).reshape((TOKENS, TOPK))
    probs = jnp.clip(0.1 + 0.9 * jax.random.uniform(key_of[3], (TOKENS, TOPK), jnp.float32) ** steps_of(key_of[3], (TOKENS, TOPK), ((0, 256),), -0.2, 0.2), 0.1, 1.0)
    w_gate = bell_draw(key_of[4], (N_EXPERT, D, FDEV), D ** -0.5, 0.09375, ((0, 32),))
    w_up = bell_draw(key_of[5], (N_EXPERT, D, FDEV), D ** -0.5, 0.09375, ((0, 32),))
    w_down = bell_draw(key_of[6], (N_EXPERT, FDEV, D), FF ** -0.5, 0.21875, ((0, 32),))
    return {"tokens": tokens, "cotangent": cotangent, "expert_ids": expert_ids, "probs": probs, "w_gate": w_gate, "w_up": w_up, "w_down": w_down}


def slot_table(expert_ids, probs):
    groups = TOKENS // TOK_DEV
    pairs = TOK_DEV * TOPK
    flat_ids = expert_ids.reshape(groups, pairs)
    onehot = (flat_ids[:, :, None] == jnp.arange(EXPERTS, dtype=jnp.int32)[None, None, :]).astype(jnp.int32)
    ranks = jnp.cumsum(onehot, axis=1) - 1
    my_rank = jnp.sum(onehot * ranks, axis=2)
    slots = flat_ids * CAP + my_rank
    token_index = (jnp.arange(groups, dtype=jnp.int32)[:, None] * TOK_DEV + jnp.arange(pairs, dtype=jnp.int32)[None, :] // TOPK)
    group_index = jnp.broadcast_to(jnp.arange(groups, dtype=jnp.int32)[:, None], (groups, pairs))
    table = jnp.zeros((groups, EXPERTS * CAP), jnp.int32).at[group_index, slots].set(token_index + 1)
    weights = jnp.zeros((groups, EXPERTS * CAP), jnp.float32).at[group_index, slots].set(probs.reshape(groups, pairs).astype(jnp.float32))
    return table, weights


def reference(tokens, cotangent, expert_ids, probs, w_gate, w_up, w_down):
    groups = TOKENS // TOK_DEV
    table, weights = slot_table(expert_ids, probs)
    total_rows = groups * CAP
    contract_last = (((1,), (1,)), ((), ()))

    def one_expert(expert, carry):
        grad_acc, gate_acc, up_acc, down_acc = carry
        ids = lax.dynamic_slice_in_dim(table, (expert * CAP).astype(jnp.int32), CAP, 1).reshape(-1)
        scales = lax.dynamic_slice_in_dim(weights, (expert * CAP).astype(jnp.int32), CAP, 1).reshape(-1)
        valid = ids > 0
        where = jnp.maximum(ids - 1, 0)
        x_rows = jnp.where(valid[:, None], tokens[where], jnp.zeros((), jnp.bfloat16))
        dy_rows = jnp.where(valid[:, None], cotangent[where], jnp.zeros((), jnp.bfloat16))
        scaled_rows = (dy_rows.astype(jnp.float32) * scales[:, None]).astype(jnp.bfloat16)
        pair_sum = jnp.zeros((total_rows, D), jnp.float32)
        for half in range(SPLIT):
            index = (expert * SPLIT + half).astype(jnp.int32)
            wg = w_gate[index]
            wu = w_up[index]
            wd = w_down[index]
            gate_pre = jnp.dot(x_rows, wg, preferred_element_type=jnp.float32)
            up_pre = jnp.dot(x_rows, wu, preferred_element_type=jnp.float32)
            sig = jax.nn.sigmoid(gate_pre)
            act = gate_pre * sig
            hidden = (act * up_pre).astype(jnp.bfloat16)
            grad_hidden = lax.dot_general(scaled_rows, wd, contract_last, preferred_element_type=jnp.float32)
            grad_gate_pre = (grad_hidden * up_pre * sig * (1.0 + gate_pre * (1.0 - sig))).astype(jnp.bfloat16)
            grad_up_pre = (grad_hidden * act).astype(jnp.bfloat16)
            row_grad = (lax.dot_general(grad_gate_pre, wg, contract_last, preferred_element_type=jnp.float32)
                        + lax.dot_general(grad_up_pre, wu, contract_last, preferred_element_type=jnp.float32)).astype(jnp.bfloat16)
            pair_sum = pair_sum + row_grad.astype(jnp.float32)
            per_dp = N_DP
            x_dp = x_rows.reshape(per_dp, total_rows // per_dp, D).astype(jnp.float32)
            s_dp = scaled_rows.reshape(per_dp, total_rows // per_dp, D).astype(jnp.float32)
            g_dp = grad_gate_pre.reshape(per_dp, total_rows // per_dp, FDEV).astype(jnp.float32)
            u_dp = grad_up_pre.reshape(per_dp, total_rows // per_dp, FDEV).astype(jnp.float32)
            h_dp = hidden.reshape(per_dp, total_rows // per_dp, FDEV).astype(jnp.float32)
            part_gate = jnp.einsum('grd,grf->gdf', x_dp, g_dp).astype(jnp.bfloat16).astype(jnp.float32)
            part_up = jnp.einsum('grd,grf->gdf', x_dp, u_dp).astype(jnp.bfloat16).astype(jnp.float32)
            part_down = jnp.einsum('grf,grd->gfd', h_dp, s_dp).astype(jnp.bfloat16).astype(jnp.float32)
            gate_acc = gate_acc.at[index].set(jnp.sum(part_gate, axis=0).astype(jnp.bfloat16))
            up_acc = up_acc.at[index].set(jnp.sum(part_up, axis=0).astype(jnp.bfloat16))
            down_acc = down_acc.at[index].set(jnp.sum(part_down, axis=0).astype(jnp.bfloat16))
        pair_grad = pair_sum.astype(jnp.bfloat16)
        grad_acc = grad_acc.at[where].add(pair_grad.astype(jnp.float32))
        return grad_acc, gate_acc, up_acc, down_acc

    start = (jnp.zeros((TOKENS, D), jnp.float32), jnp.zeros((N_EXPERT, D, FDEV), jnp.bfloat16),
             jnp.zeros((N_EXPERT, D, FDEV), jnp.bfloat16), jnp.zeros((N_EXPERT, FDEV, D), jnp.bfloat16))
    grad_acc, gate_acc, up_acc, down_acc = lax.fori_loop(0, EXPERTS, one_expert, start)
    return grad_acc.astype(jnp.bfloat16), gate_acc, up_acc, down_acc
```

```python
import jax
import jax.numpy as jnp
from jax import lax
from jax.experimental import pallas as pl
from jax.experimental.pallas import tpu as pltpu
from jax.sharding import PartitionSpec as P

D = 4096
F = 384
TOK = 128
N_DP = 8
CHIPS = 16
J = 8
DS = D // J
MAIN = 16
HALF = CHIPS * MAIN
ROWS = 2 * HALF + 64
UNIT = 96
MESH = pl.DeviceIdType.MESH
F32 = jnp.float32
BF16 = jnp.bfloat16
OTHERS = (
    (0, 1), (1, 0), (0, 3), (3, 0), (1, 1), (3, 3), (1, 3), (3, 1),
    (0, 2), (2, 0), (2, 1), (1, 2), (2, 3), (3, 2), (2, 2),
)
X_AT, XE_AT, S_AT, SE_AT, R_AT, RE_AT = 0, 4, 5, 13, 14, 18
RG_AT, RGE_AT = 14, 22


def mm(a, b):
    return jnp.dot(a, b, preferred_element_type=F32)


def mm_nt(a, b):
    return lax.dot_general(a, b, (((1,), (1,)), ((), ())), preferred_element_type=F32)


def iota(shape, dim):
    return lax.broadcasted_iota(jnp.int32, shape, dim)


def eye(n):
    return (iota((n, n), 0) == iota((n, n), 1)).astype(BF16)


def kernel(
    ids, probs, tok, cot, wg, wu, wd,
    gt, grads,
    tokb, cotb, w_gu, w_d, xs, xse, ss, sse, X, XE, S, SE,
    pick, pick_e, pick_t, pick_et, scales, pre, gh, ggu, at,
    RG, RGE, RV, RVE, PS, PSE, RT, RTE, ring, gts, gds,
    loc, snd, rcv, sib_s, sib_r, ring_s, ring_r,
):
    z = lax.axis_index("dp")
    e = lax.axis_index("expert")
    k = lax.rem(e, 2)
    c = e // 2
    cy = c // 4
    cx = lax.rem(c, 4)
    sibling = (z, c * 2 + (1 - k))
    z_next = (lax.rem(z + 1, N_DP), e)
    z_prev = (lax.rem(z + N_DP - 1, N_DP), e)
    chip_of = [lax.rem(cy + dy, 4) * 4 + lax.rem(cx + dx, 4) for dy, dx in OTHERS]

    for j in range(J):
        cols = pl.ds(j * DS, DS)
        pltpu.make_async_copy(tok.at[:, cols], tokb.at[j], loc.at[0]).start()
    for j in range(J):
        cols = pl.ds(j * DS, DS)
        pltpu.make_async_copy(cot.at[:, cols], cotb.at[j], loc.at[1]).start()
    barrier = pltpu.get_barrier_semaphore()
    for chip in chip_of:
        pl.semaphore_signal(barrier, inc=1, device_id=(z, chip * 2 + k), device_id_type=MESH)
    for dev in (sibling, z_next, z_prev):
        pl.semaphore_signal(barrier, inc=1, device_id=dev, device_id_type=MESH)
    for j in range(J):
        rows = pl.ds(j * DS, DS)
        pltpu.make_async_copy(wg.at[rows, :], w_gu.at[j, :, pl.ds(0, F)], loc.at[2]).start()
        pltpu.make_async_copy(wu.at[rows, :], w_gu.at[j, :, pl.ds(F, F)], loc.at[2]).start()
    for j in range(J):
        pltpu.make_async_copy(wd.at[:, pl.ds(j * DS, DS)], w_d.at[j], loc.at[3]).start()

    def wait_bytes(ref, sem):
        pltpu.make_async_copy(ref, ref, sem).wait()

    id0, id1 = ids[0:1, :], ids[1:2, :]
    p0, p1 = probs[0:1, :], probs[1:2, :]
    row = iota((HALF, TOK), 0)
    expert, slot = row // MAIN, lax.rem(row, MAIN)
    named0, named1 = id0 == expert, id1 == expert
    named = named0 | named1
    before = (iota((TOK, TOK), 0) < iota((TOK, TOK), 1)).astype(BF16)
    rank = mm(named.astype(F32).astype(BF16), before).astype(jnp.int32)
    main = named & (rank == slot)
    extra = named & (rank == MAIN + lax.rem(slot, 2))
    pick[...] = main.astype(F32).astype(BF16)
    pick_e[...] = extra.astype(F32).astype(BF16)

    def scale_of(picked):
        each = jnp.where(picked & named0, p0, 0.0) + jnp.where(picked & named1, p1, 0.0)
        return jnp.broadcast_to(jnp.sum(each, axis=1, keepdims=True), (HALF, TOK))

    scales[0] = scale_of(main)
    scales[1] = scale_of(extra)
    part = lax.rem(iota((HALF, TOK), 0), MAIN) // 2

    def extras_of(source):
        def add(j, total):
            chosen = jnp.where(part == j, pick_e[...].astype(F32), 0.0).astype(BF16)
            return total + mm(chosen, source[j])
        return lax.fori_loop(0, J, add, jnp.zeros((HALF, DS), F32))

    def blk(i):
        return pl.ds(pl.multiple_of(i * MAIN, MAIN), MAIN)

    def home(i):
        return pl.ds(pl.multiple_of(k * HALF + i * MAIN, MAIN), MAIN)

    mine = pl.ds(pl.multiple_of(k * HALF, HALF), HALF)
    theirs = pl.ds(pl.multiple_of((1 - k) * HALF, HALF), HALF)

    def send_all(src_of, dst, at_sem):
        for chip in chip_of:
            pltpu.make_async_remote_copy(
                src_ref=src_of(chip), dst_ref=dst,
                send_sem=snd.at[at_sem], recv_sem=rcv.at[at_sem],
                device_id=(z, chip * 2 + k), device_id_type=MESH,
            ).start()
        pltpu.make_async_copy(src_of(c), dst, rcv.at[at_sem]).start()

    def to_sibling(src, dst, at_sem):
        return pltpu.make_async_remote_copy(
            src_ref=src, dst_ref=dst, send_sem=sib_s.at[at_sem], recv_sem=sib_r.at[at_sem],
            device_id=sibling, device_id_type=MESH,
        )

    wait_bytes(tokb, loc.at[0])
    xse[...] = extras_of(tokb).astype(BF16)
    pl.semaphore_wait(barrier, len(OTHERS) + 3)
    send_all(lambda i: xse.at[blk(i), :], XE.at[home(c), :], XE_AT)

    @pl.loop(0, 4)
    def _(q):
        for n in range(2):
            xs[2 * q + n] = mm(pick[...], tokb[2 * q + n]).astype(BF16)
        two = pl.ds(2 * q, 2)
        send_all(lambda i: xs.at[two, blk(i), :], X.at[two, home(c), :], X_AT + q)

    wait_bytes(cotb, loc.at[1])
    sse[...] = (extras_of(cotb) * scales[1][:, 0:1]).astype(BF16)
    pick_t[...] = mm_nt(eye(TOK), pick[...]).astype(BF16)
    pick_et[...] = mm_nt(eye(TOK), pick_e[...]).astype(BF16)
    for u in range(12):
        ring[u, 0] = jnp.zeros((UNIT, DS), BF16)
    pre[...] = jnp.zeros_like(pre)
    gh[...] = jnp.zeros_like(gh)

    def order(i):
        pair = i // 2
        first = lax.rem(z + 15 - pair, N_DP)
        second = lax.rem(z + 1 + pair + 4 * (pair // 3), N_DP)
        odd = lax.rem(i, 2)
        return first * (1 - odd) + second * odd

    def send_cot(i):
        o = order(i)
        ss[o] = (mm(pick[...], cotb[o]) * scales[0][:, 0:1]).astype(BF16)
        send_all(lambda n: ss.at[o, blk(n), :], S.at[o, home(c), :], S_AT + i)

    def unpack(j):
        r, col = iota((64, 2 * HALF), 0), iota((64, 2 * HALF), 1)
        return (col == (r // 2) * MAIN + 2 * j + lax.rem(r, 2)).astype(F32).astype(BF16)

    def unpack_t(j):
        r, col = iota((2 * HALF, 64), 1), iota((2 * HALF, 64), 0)
        return (col == (r // 2) * MAIN + 2 * j + lax.rem(r, 2)).astype(F32).astype(BF16)

    tail = pl.ds(2 * HALF, 64)

    wait_bytes(XE.at[pl.ds(0, HALF), :], rcv.at[XE_AT])
    fwd_xe = to_sibling(XE.at[mine, :], XE.at[mine, :], XE_AT)
    fwd_xe.start()
    fwd_xe.wait_recv()

    @pl.loop(0, J)
    def _(j):
        X[j, tail, :] = mm(unpack(j), XE[...]).astype(BF16)

    send_all(lambda i: sse.at[blk(i), :], SE.at[home(c), :], SE_AT)
    wait_bytes(w_gu, loc.at[2])

    @pl.loop(0, 4)
    def _(q):
        two = pl.ds(2 * q, 2)
        wait_bytes(X.at[two, pl.ds(0, HALF), :], rcv.at[X_AT + q])
        fwd = to_sibling(X.at[two, mine, :], X.at[two, mine, :], X_AT + q)
        fwd.start()
        send_cot(2 * q)
        send_cot(2 * q + 1)
        fwd.wait_recv()
        pre[...] += mm(X[2 * q], w_gu[2 * q]) + mm(X[2 * q + 1], w_gu[2 * q + 1])

    def store_t(first, value):
        at[pl.ds(first, F), :] = mm_nt(eye(F), value).astype(BF16)

    gate, up = pre[:, 0:F], pre[:, F:2 * F]
    store_t(2 * F, (gate * jax.nn.sigmoid(gate) * up).astype(BF16))

    def ring_step(t, forward, group, source):
        u0, units, first = group
        d = lax.rem(z + 15 - t, N_DP) if forward else lax.rem(z + 1 + t, N_DP)
        part_sum = mm(at[pl.ds(first, units * UNIT), :], source[d])
        for n in range(units):
            u = u0 + n
            slot_ref = ring.at[u, t]

            @pl.when(t > 0)
            def _():
                wait_bytes(slot_ref, ring_r.at[u, t])

            total = (part_sum[n * UNIT:(n + 1) * UNIT] + slot_ref[...].astype(F32)).astype(BF16)

            @pl.when(t < N_DP - 1)
            def _():
                slot_ref[...] = total
                pltpu.make_async_remote_copy(
                    src_ref=slot_ref, dst_ref=ring.at[u, t + 1],
                    send_sem=ring_s.at[u, t], recv_sem=ring_r.at[u, t + 1],
                    device_id=z_next if forward else z_prev, device_id_type=MESH,
                ).start()

            @pl.when(t == N_DP - 1)
            def _():
                gds[pl.ds(first + n * UNIT, UNIT), :] = total

    def ring_down(t):
        ring_step(t, True, (0, 2, 2 * F), S)
        ring_step(t, False, (2, 2, 2 * F + 192), S)

    def ring_gate_up(t):
        ring_step(t, True, (4, 4, 0), X)
        ring_step(t, False, (8, 4, F), X)

    wait_bytes(SE.at[pl.ds(0, HALF), :], rcv.at[SE_AT])
    fwd_se = to_sibling(SE.at[mine, :], SE.at[mine, :], SE_AT)
    fwd_se.start()
    fwd_se.wait_recv()
    wait_bytes(w_d, loc.at[3])

    @pl.loop(0, 4)
    def _(pair):
        for n in range(2):
            i = 2 * pair + n
            o = order(i)
            wait_bytes(S.at[o, pl.ds(0, HALF), :], rcv.at[S_AT + i])
            to_sibling(S.at[o, mine, :], S.at[o, mine, :], S_AT + i).start()
        for n in range(2):
            i = 2 * pair + n
            o = order(i)
            S[o, tail, :] = mm(unpack(o), SE[...]).astype(BF16)
            to_sibling(S.at[o, mine, :], S.at[o, mine, :], S_AT + i).wait_recv()
        ring_down(pair)
        for n in range(2):
            o = order(2 * pair + n)
            gh[...] += mm_nt(S[o], w_d[o])

    gate, up, grad = pre[:, 0:F], pre[:, F:2 * F], gh[...]
    sig = jax.nn.sigmoid(gate)
    ggate = (grad * up * sig * (1.0 + gate * (1.0 - sig))).astype(BF16)
    gup = (grad * gate * sig).astype(BF16)
    ggu[:, 0:F] = ggate
    ggu[:, F:2 * F] = gup
    store_t(0, ggate)
    store_t(F, gup)

    def row_grad(j):
        RG[j] = mm_nt(ggu[...], w_gu[j]).astype(BF16)
        to_sibling(RG.at[j, theirs, :], RV.at[j], RG_AT + j).start()

    def pair_grad(q):
        for n in range(2):
            j = 2 * q + n
            to_sibling(RG.at[j, theirs, :], RV.at[j], RG_AT + j).wait_recv()
            PS[j] = (RG[j, mine, :].astype(F32) + RV[j].astype(F32)).astype(BF16)
        two = pl.ds(2 * q, 2)
        send_all(lambda i: PS.at[two, blk(i), :], RT.at[two, blk(c), :], R_AT + q)

    def row_grad_extras():
        def add(j, total):
            return total + mm(unpack_t(j), RG[j, tail, :])
        RGE[...] = lax.fori_loop(0, J, add, jnp.zeros((2 * HALF, DS), F32)).astype(BF16)
        to_sibling(RGE.at[theirs, :], RVE, RGE_AT).start()

    def pair_grad_extras():
        to_sibling(RGE.at[theirs, :], RVE, RGE_AT).wait_recv()
        PSE[...] = (RGE[mine, :].astype(F32) + RVE[...].astype(F32)).astype(BF16)
        send_all(lambda i: PSE.at[blk(i), :], RTE.at[blk(c), :], RE_AT)

    part_col = lax.rem(iota((TOK, HALF), 1), MAIN) // 2

    def token_grad(q):
        two = pl.ds(2 * q, 2)
        wait_bytes(RT.at[two], rcv.at[R_AT + q])
        for n in range(2):
            j = 2 * q + n
            chosen = jnp.where(part_col == j, pick_et[...].astype(F32), 0.0).astype(BF16)
            gts[j] = (mm(pick_t[...], RT[j]) + mm(chosen, RTE[...])).astype(BF16)
            pltpu.make_async_copy(gts.at[j], gt.at[j], loc.at[4]).start()

    @pl.loop(0, N_DP)
    def _(t):
        ring_gate_up(t)

        @pl.when(t < 4)
        def _():
            ring_down(t + 4)
            row_grad(2 * t)
            row_grad(2 * t + 1)

        @pl.when((t > 0) & (t < 5))
        def _():
            pair_grad(t - 1)

        @pl.when(t == 4)
        def _():
            row_grad_extras()

        @pl.when(t == 5)
        def _():
            pair_grad_extras()

        @pl.when(t == 6)
        def _():
            wait_bytes(RTE, rcv.at[RE_AT])

            @pl.loop(0, 4)
            def _(q):
                token_grad(q)

    out = pltpu.make_async_copy(gds, grads, loc.at[5])
    out.start()

    def sent(ref, sem):
        wait_bytes(ref, sem)

    less = HALF - MAIN
    for q in range(4):
        two = pl.ds(2 * q, 2)
        sent(xs.at[two, pl.ds(0, less), :], snd.at[X_AT + q])
        sent(PS.at[two, pl.ds(0, less), :], snd.at[R_AT + q])
        sent(X.at[two, pl.ds(0, HALF), :], sib_s.at[X_AT + q])
    for i in range(J):
        sent(ss.at[i, pl.ds(0, less), :], snd.at[S_AT + i])
        sent(ss.at[i], sib_s.at[S_AT + i])
        sent(RV.at[i], sib_s.at[RG_AT + i])
    for at_sem in (XE_AT, SE_AT, RE_AT):
        sent(xse.at[pl.ds(0, less), :], snd.at[at_sem])
    for at_sem in (XE_AT, SE_AT, RGE_AT):
        sent(xse, sib_s.at[at_sem])

    @pl.loop(0, N_DP - 1)
    def _(t):
        for u in range(12):
            sent(ring.at[u, t], ring_s.at[u, t])

    wait_bytes(gts, loc.at[4])
    out.wait()


def shards(tokens, cotangent, expert_ids, probs, w_gate, w_up, w_down):
    any_ = pl.BlockSpec(memory_space=pl.ANY)
    vmem = pl.BlockSpec(memory_space=pltpu.VMEM)
    dma = pltpu.SemaphoreType.DMA
    v = pltpu.VMEM
    gt, grads = pl.pallas_call(
        kernel,
        out_shape=(
            jax.ShapeDtypeStruct((J, TOK, DS), BF16),
            jax.ShapeDtypeStruct((3 * F, DS), BF16),
        ),
        in_specs=[vmem, vmem] + [any_] * 5,
        out_specs=(any_, any_),
        scratch_shapes=[
            v((J, TOK, DS), BF16), v((J, TOK, DS), BF16),
            v((J, DS, 2 * F), BF16), v((J, F, DS), BF16),
            v((J, HALF, DS), BF16), v((HALF, DS), BF16),
            v((J, HALF, DS), BF16), v((HALF, DS), BF16),
            v((J, ROWS, DS), BF16), v((2 * HALF, DS), BF16),
            v((J, ROWS, DS), BF16), v((2 * HALF, DS), BF16),
            v((HALF, TOK), BF16), v((HALF, TOK), BF16),
            v((TOK, HALF), BF16), v((TOK, HALF), BF16),
            v((2, HALF, TOK), F32),
            v((ROWS, 2 * F), F32), v((ROWS, F), F32),
            v((ROWS, 2 * F), BF16), v((3 * F, ROWS), BF16),
            v((J, ROWS, DS), BF16), v((2 * HALF, DS), BF16),
            v((J, HALF, DS), BF16), v((HALF, DS), BF16),
            v((J, HALF, DS), BF16), v((HALF, DS), BF16),
            v((J, HALF, DS), BF16), v((HALF, DS), BF16),
            v((12, N_DP, UNIT, DS), BF16),
            v((J, TOK, DS), BF16), v((3 * F, DS), BF16),
            dma((6,)), dma((19,)), dma((19,)), dma((23,)), dma((23,)),
            dma((12, N_DP)), dma((12, N_DP)),
        ],
        compiler_params=pltpu.CompilerParams(
            collective_id=0, has_side_effects=True, vmem_limit_bytes=60 * 2**20
        ),
        cost_estimate=pl.CostEstimate(
            flops=15_000_000_000, bytes_accessed=14_000_000, transcendentals=500_000
        ),
    )(expert_ids.T, probs.T, tokens, cotangent, w_gate[0], w_up[0], w_down[0])
    return (
        gt.transpose(1, 0, 2).reshape(TOK, D),
        grads[0:F].T[None],
        grads[F:2 * F].T[None],
        grads[2 * F:][None],
    )


def solution(mesh):
    in_specs = (
        P(("dp", "expert"), None),
        P(("dp", "expert"), None),
        P(("dp", "expert"), None),
        P(("dp", "expert"), None),
        P("expert", None, None),
        P("expert", None, None),
        P("expert", None, None),
    )
    out_specs = (
        P(("dp", "expert"), None),
        P("expert", "dp", None),
        P("expert", "dp", None),
        P("expert", None, "dp"),
    )
    return jax.shard_map(shards, mesh=mesh, in_specs=in_specs, out_specs=out_specs, check_vma=False)
```

```python
import jax
import jax.numpy as jnp
from jax import lax
from jax.experimental import pallas as pl
from jax.experimental.pallas import tpu as pltpu
from jax.sharding import PartitionSpec as P

D = 4096
F = 384
TOK = 128
N_DP = 8
CHIPS = 16
J = 8
DS = D // J
MAIN = 16
HALF = CHIPS * MAIN
ROWS = 2 * HALF + 64
UNIT = 96
MESH = pl.DeviceIdType.MESH
F32 = jnp.float32
BF16 = jnp.bfloat16
OTHERS = (
    (0, 1), (1, 0), (0, 3), (3, 0), (1, 1), (3, 3), (1, 3), (3, 1),
    (0, 2), (2, 0), (2, 1), (1, 2), (2, 3), (3, 2), (2, 2),
)
X_AT, XE_AT, S_AT, SE_AT, R_AT, RE_AT = 0, 8, 9, 17, 18, 22
RG_AT, RGE_AT = 18, 26
LAG = 2


def mm(a, b):
    return jnp.dot(a, b, preferred_element_type=F32)


def mm_nt(a, b):
    return lax.dot_general(a, b, (((1,), (1,)), ((), ())), preferred_element_type=F32)


def iota(shape, dim):
    return lax.broadcasted_iota(jnp.int32, shape, dim)


def eye(n):
    return (iota((n, n), 0) == iota((n, n), 1)).astype(BF16)


def kernel(
    ids, probs, tok, cot, wg, wu, wd,
    gt, gg, gu, gd,
    tokb, cotb, w_gu, w_d, xs, xse, ss, sse, X, XE, S, SE,
    pick, pick_e, pick_t, pick_et, scales, pre, gh, ggu, at,
    RG, RGE, RV, RVE, PS, PSE, RT, RTE, ring, begin, psum, gds, outs,
    loc, snd, rcv, sib_s, sib_r, ring_s, ring_r,
):
    z = lax.axis_index("dp")
    e = lax.axis_index("expert")
    k = lax.rem(e, 2)
    c = e // 2
    cy = c // 4
    cx = lax.rem(c, 4)
    sibling = (z, c * 2 + (1 - k))
    z_next = (lax.rem(z + 1, N_DP), e)
    z_prev = (lax.rem(z + N_DP - 1, N_DP), e)
    chip_of = [lax.rem(cy + dy, 4) * 4 + lax.rem(cx + dx, 4) for dy, dx in OTHERS]

    barrier = pltpu.get_barrier_semaphore()
    for dev in (z_next, z_prev):
        pl.semaphore_signal(barrier, inc=1, device_id=dev, device_id_type=MESH)
    for chip in chip_of:
        pl.semaphore_signal(barrier, inc=1, device_id=(z, chip * 2 + k), device_id_type=MESH)
    pl.semaphore_signal(barrier, inc=1, device_id=sibling, device_id_type=MESH)
    for j in range(J):
        pltpu.make_async_copy(tok.at[:, pl.ds(j * DS, DS)], tokb.at[j], loc.at[0]).start()

    def wait_bytes(ref, sem):
        pltpu.make_async_copy(ref, ref, sem).wait()

    id0, id1 = ids[0:1, :], ids[1:2, :]
    p0, p1 = probs[0:1, :], probs[1:2, :]
    row = iota((HALF, TOK), 0)
    expert, slot = row // MAIN, lax.rem(row, MAIN)
    named0, named1 = id0 == expert, id1 == expert
    named = named0 | named1
    before = (iota((TOK, TOK), 0) < iota((TOK, TOK), 1)).astype(BF16)
    rank = mm(named.astype(F32).astype(BF16), before).astype(jnp.int32)
    main = named & (rank == slot)
    extra = named & (rank == MAIN + lax.rem(slot, 2))
    pick[...] = main.astype(F32).astype(BF16)
    pick_e[...] = extra.astype(F32).astype(BF16)

    def scale_of(picked):
        each = jnp.where(picked & named0, p0, 0.0) + jnp.where(picked & named1, p1, 0.0)
        return jnp.broadcast_to(jnp.sum(each, axis=1, keepdims=True), (HALF, TOK))

    scales[0] = scale_of(main)
    scales[1] = scale_of(extra)
    part = lax.rem(iota((HALF, TOK), 0), MAIN) // 2

    def extras_of(source):
        def add(j, total):
            chosen = jnp.where(part == j, pick_e[...].astype(F32), 0.0).astype(BF16)
            return total + mm(chosen, source[j])
        return lax.fori_loop(0, J, add, jnp.zeros((HALF, DS), F32))

    def blk(i):
        return pl.ds(pl.multiple_of(i * MAIN, MAIN), MAIN)

    def home(i):
        return pl.ds(pl.multiple_of(k * HALF + i * MAIN, MAIN), MAIN)

    mine = pl.ds(pl.multiple_of(k * HALF, HALF), HALF)
    theirs = pl.ds(pl.multiple_of((1 - k) * HALF, HALF), HALF)

    def send_all(src_of, dst, at_sem):
        for chip in chip_of:
            pltpu.make_async_remote_copy(
                src_ref=src_of(chip), dst_ref=dst,
                send_sem=snd.at[at_sem], recv_sem=rcv.at[at_sem],
                device_id=(z, chip * 2 + k), device_id_type=MESH,
            ).start()
        pltpu.make_async_copy(src_of(c), dst, rcv.at[at_sem]).start()

    def to_sibling(src, dst, at_sem):
        return pltpu.make_async_remote_copy(
            src_ref=src, dst_ref=dst, send_sem=sib_s.at[at_sem], recv_sem=sib_r.at[at_sem],
            device_id=sibling, device_id_type=MESH,
        )

    wait_bytes(tokb, loc.at[0])

    def send_tok(j):
        send_all(lambda i: xs.at[j, blk(i), :], X.at[j, home(c), :], X_AT + j)

    xs[0] = mm(pick[...], tokb[0]).astype(BF16)
    pl.semaphore_wait(barrier, len(OTHERS) + 3)
    send_tok(0)
    xse[...] = extras_of(tokb).astype(BF16)
    send_all(lambda i: xse.at[blk(i), :], XE.at[home(c), :], XE_AT)

    @pl.loop(1, J)
    def _(j):
        xs[j] = mm(pick[...], tokb[j]).astype(BF16)
        send_tok(j)

    for j in range(J):
        pltpu.make_async_copy(cot.at[:, pl.ds(j * DS, DS)], cotb.at[j], loc.at[1]).start()
    for j in range(J):
        rows = pl.ds(j * DS, DS)
        pltpu.make_async_copy(wg.at[rows, :], w_gu.at[j, :, pl.ds(0, F)], loc.at[2]).start()
        pltpu.make_async_copy(wu.at[rows, :], w_gu.at[j, :, pl.ds(F, F)], loc.at[2]).start()
    for j in range(J):
        pltpu.make_async_copy(wd.at[:, pl.ds(j * DS, DS)], w_d.at[j], loc.at[3]).start()

    wait_bytes(cotb, loc.at[1])
    sse[...] = (extras_of(cotb) * scales[1][:, 0:1]).astype(BF16)
    pick_t[...] = mm_nt(eye(TOK), pick[...]).astype(BF16)
    pick_et[...] = mm_nt(eye(TOK), pick_e[...]).astype(BF16)
    pre[...] = jnp.zeros_like(pre)
    gh[...] = jnp.zeros_like(gh)

    def place(t, up):
        return lax.rem(z + 12 - t, N_DP) if up else lax.rem(z + 4 + t, N_DP)

    def order(i):
        odd = lax.rem(i, 2)
        return place((i + 1) // 2, True) * odd + place(i // 2, False) * (1 - odd)

    def send_cot(i):
        o = order(i)
        ss[o] = (mm(pick[...], cotb[o]) * scales[0][:, 0:1]).astype(BF16)
        send_all(lambda n: ss.at[o, blk(n), :], S.at[o, home(c), :], S_AT + i)

    def unpack(j):
        r, col = iota((64, 2 * HALF), 0), iota((64, 2 * HALF), 1)
        return (col == (r // 2) * MAIN + 2 * j + lax.rem(r, 2)).astype(F32).astype(BF16)

    def unpack_t(j):
        r, col = iota((2 * HALF, 64), 1), iota((2 * HALF, 64), 0)
        return (col == (r // 2) * MAIN + 2 * j + lax.rem(r, 2)).astype(F32).astype(BF16)

    tail = pl.ds(2 * HALF, 64)

    wait_bytes(XE.at[pl.ds(0, HALF), :], rcv.at[XE_AT])
    fwd_xe = to_sibling(XE.at[mine, :], XE.at[mine, :], XE_AT)
    fwd_xe.start()
    fwd_xe.wait_recv()

    @pl.loop(0, J)
    def _(j):
        X[j, tail, :] = mm(unpack(j), XE[...]).astype(BF16)

    send_all(lambda i: sse.at[blk(i), :], SE.at[home(c), :], SE_AT)
    wait_bytes(w_gu, loc.at[2])

    @pl.loop(0, J)
    def _(j):
        wait_bytes(X.at[j, pl.ds(0, HALF), :], rcv.at[X_AT + j])
        fwd = to_sibling(X.at[j, mine, :], X.at[j, mine, :], X_AT + j)
        fwd.start()

        @pl.when(j >= LAG)
        def _():
            send_cot(j - LAG)

        fwd.wait_recv()
        pre[...] += mm(X[j], w_gu[j])

    @pl.loop(J - LAG, J)
    def _(i):
        send_cot(i)

    def store_t(first, value):
        at[pl.ds(first, F), :] = mm_nt(eye(F), value).astype(BF16)

    gate, up = pre[:, 0:F], pre[:, F:2 * F]
    store_t(2 * F, (gate * jax.nn.sigmoid(gate) * up).astype(BF16))

    def pass_on(v, t, src, up):
        pltpu.make_async_remote_copy(
            src_ref=src, dst_ref=ring.at[v, t],
            send_sem=ring_s.at[v, t], recv_sem=ring_r.at[v, t],
            device_id=z_next if up else z_prev, device_id_type=MESH,
        ).start()

    down, gate_up = (0, 4, 2 * F), (4, 8, 0)

    def begin_chains(group, source):
        u0, n, first = group
        terms = mm(at[pl.ds(first, n * UNIT), :], source[place(0, False)])
        for m in range(n):
            begin[u0 + m] = terms[m * UNIT:(m + 1) * UNIT].astype(BF16)

        @pl.loop(0, n // 2)
        def _(m):
            pass_on(u0 + m, 0, begin.at[u0 + m], False)
            pass_on(12 + u0 + n // 2 + m, 0, begin.at[u0 + n // 2 + m], True)

    def terms_of(group, t, up, source):
        u0, n, first = group
        terms = mm(at[pl.ds(first, n * UNIT), :], source[place(t, up)])
        for m in range(n):
            psum[up * 8 + m] = terms[m * UNIT:(m + 1) * UNIT]

    def hop(group, m, t, up, joins):
        v = up * 12 + group[0] + m
        slot_ref = ring.at[v, t - 1]
        if joins:
            wait_bytes(slot_ref, ring_r.at[v, t - 1])
            slot_ref[...] = (psum[up * 8 + m] + slot_ref[...].astype(F32)).astype(BF16)
        else:
            slot_ref[...] = psum[up * 8 + m].astype(BF16)
        pass_on(v, t, slot_ref, up)

    def hops(group, t, half, ups):
        n = group[1]

        @pl.loop(0, n // 2)
        def _(m):
            joins = t > 1 or half == 1
            for up in ups:
                upper = (half == 0) != bool(up)
                hop(group, m + (n // 2 if upper else 0), t, up, joins)

    def end_chains(group, source):
        u0, n, first = group
        terms_of(group, 4, 0, source)

        def end(m):
            for up in range(2):
                wait_bytes(ring.at[up * 12 + u0 + m, 3], ring_r.at[up * 12 + u0 + m, 3])
            came = ring[u0 + m, 3].astype(F32) + ring[12 + u0 + m, 3].astype(F32)
            rows = pl.ds(pl.multiple_of(first + m * UNIT, UNIT), UNIT)
            gds[rows, :] = (psum[m] + came).astype(BF16)

        @pl.loop(0, n // 2)
        def _(m):
            end(m)
            end(n // 2 + m)

    wait_bytes(SE.at[pl.ds(0, HALF), :], rcv.at[SE_AT])
    fwd_se = to_sibling(SE.at[mine, :], SE.at[mine, :], SE_AT)
    fwd_se.start()
    fwd_se.wait_recv()
    wait_bytes(w_d, loc.at[3])

    def forward(i):
        o = order(i)
        wait_bytes(S.at[o, pl.ds(0, HALF), :], rcv.at[S_AT + i])
        to_sibling(S.at[o, mine, :], S.at[o, mine, :], S_AT + i).start()
        S[o, tail, :] = mm(unpack(o), SE[...]).astype(BF16)

    def here(i):
        o = order(i)
        to_sibling(S.at[o, mine, :], S.at[o, mine, :], S_AT + i).wait_recv()

    def grad_hidden(i):
        o = order(i)
        gh[...] += mm_nt(S[o], w_d[o])

    def down_step(t, up):
        terms_of(down, t, up, S)
        hops(down, t, 0, (up,))
        hops(down, t, 1, (up,))

    forward(0)
    here(0)
    begin_chains(down, S)
    for i in range(1, 7):
        forward(i)
        grad_hidden(i - 1)
        here(i)
        if i == 6:
            forward(7)
        down_step((i + 1) // 2, i % 2)
    grad_hidden(6)
    here(7)
    grad_hidden(7)

    gate, up, grad = pre[:, 0:F], pre[:, F:2 * F], gh[...]
    sig = jax.nn.sigmoid(gate)
    ggate = (grad * up * sig * (1.0 + gate * (1.0 - sig))).astype(BF16)
    gup = (grad * gate * sig).astype(BF16)
    ggu[:, 0:F] = ggate
    ggu[:, F:2 * F] = gup
    store_t(0, ggate)
    store_t(F, gup)

    def row_grad(j):
        RG[j] = mm_nt(ggu[...], w_gu[j]).astype(BF16)
        to_sibling(RG.at[j, theirs, :], RV.at[j], RG_AT + j).start()

    def pair_grad(q):
        for n in range(2):
            j = 2 * q + n
            to_sibling(RG.at[j, theirs, :], RV.at[j], RG_AT + j).wait_recv()
            PS[j] = (RG[j, mine, :].astype(F32) + RV[j].astype(F32)).astype(BF16)
        two = pl.ds(2 * q, 2)
        send_all(lambda i: PS.at[two, blk(i), :], RT.at[two, blk(c), :], R_AT + q)

    def row_grad_extras():
        def add(j, total):
            return total + mm(unpack_t(j), RG[j, tail, :])
        RGE[...] = lax.fori_loop(0, J, add, jnp.zeros((2 * HALF, DS), F32)).astype(BF16)
        to_sibling(RGE.at[theirs, :], RVE, RGE_AT).start()

    def pair_grad_extras():
        to_sibling(RGE.at[theirs, :], RVE, RGE_AT).wait_recv()
        PSE[...] = (RGE[mine, :].astype(F32) + RVE[...].astype(F32)).astype(BF16)
        send_all(lambda i: PSE.at[blk(i), :], RTE.at[blk(c), :], RE_AT)

    part_col = lax.rem(iota((TOK, HALF), 1), MAIN) // 2

    def token_grad(q):
        two = pl.ds(2 * q, 2)
        wait_bytes(RT.at[two], rcv.at[R_AT + q])
        for n in range(2):
            j = 2 * q + n
            chosen = jnp.where(part_col == j, pick_et[...].astype(F32), 0.0).astype(BF16)
            tokb[j] = (mm(pick_t[...], RT[j]) + mm(chosen, RTE[...])).astype(BF16)
            cols = pl.ds(pl.multiple_of(j * DS, DS), DS)
            pltpu.make_async_copy(tokb.at[j], gt.at[:, cols], loc.at[4]).start()

    def several(first, last, what):
        @pl.loop(first, last)
        def _(n):
            what(n)

    begin_chains(gate_up, X)
    several(0, 4, row_grad)
    for t in range(1, 4):
        terms_of(gate_up, t, 1, X)
        terms_of(gate_up, t, 0, X)
        hops(gate_up, t, 0, (1, 0))
        if t == 1:
            several(4, 8, row_grad)
            pair_grad(0)
            pair_grad(1)
        if t == 2:
            pair_grad_extras()
        hops(gate_up, t, 1, (1, 0))
        if t == 1:
            several(2, 4, pair_grad)
            row_grad_extras()
    end_chains(down, S)
    pltpu.make_async_copy(gds.at[pl.ds(2 * F, F), :], gd, loc.at[5]).start()
    wait_bytes(RTE, rcv.at[RE_AT])
    several(0, 4, token_grad)
    end_chains(gate_up, X)
    out_d = pltpu.make_async_copy(gds.at[pl.ds(2 * F, F), :], gd, loc.at[5])
    for n, dst in enumerate((gg, gu)):
        outs[n] = mm_nt(eye(DS), gds[n * F:(n + 1) * F, :]).astype(BF16)
        pltpu.make_async_copy(outs.at[n], dst, loc.at[6 + n]).start()

    def sent(ref, sem):
        wait_bytes(ref, sem)

    less = HALF - MAIN
    for q in range(4):
        two = pl.ds(2 * q, 2)
        sent(PS.at[two, pl.ds(0, less), :], snd.at[R_AT + q])
    for i in range(J):
        sent(xs.at[i, pl.ds(0, less), :], snd.at[X_AT + i])
        sent(ss.at[i, pl.ds(0, less), :], snd.at[S_AT + i])
        sent(xs.at[i], sib_s.at[X_AT + i])
        sent(ss.at[i], sib_s.at[S_AT + i])
        sent(RV.at[i], sib_s.at[RG_AT + i])
    for at_sem in (XE_AT, SE_AT, RE_AT):
        sent(xse.at[pl.ds(0, less), :], snd.at[at_sem])
    for at_sem in (XE_AT, SE_AT, RGE_AT):
        sent(xse, sib_s.at[at_sem])

    @pl.loop(0, 24)
    def _(v):
        for t in range(1, 4):
            sent(ring.at[v, t], ring_s.at[v, t])

    for u0, n, _ in (down, gate_up):
        for m in range(n // 2):
            sent(begin.at[0], ring_s.at[u0 + m, 0])
            sent(begin.at[0], ring_s.at[12 + u0 + n // 2 + m, 0])

    wait_bytes(tokb, loc.at[4])
    out_d.wait()
    for n, dst in enumerate((gg, gu)):
        pltpu.make_async_copy(outs.at[n], dst, loc.at[6 + n]).wait()


def write_out(gt, gg, gu, gd, gt_out, gg_out, gu_out, gd_out, gt_v, gg_v, gu_v, gd_v, sem):
    whole = ((gg, gg_v, gg_out), (gu, gu_v, gu_out), (gd, gd_v, gd_out))
    parts = [tuple(ref.at[pl.ds(32 * n, 32), :] for ref in (gt, gt_v, gt_out)) for n in range(4)]
    parts += whole
    reads = [pltpu.make_async_copy(src, mid, sem.at[0, n]) for n, (src, mid, _) in enumerate(parts)]
    writes = [pltpu.make_async_copy(mid, dst, sem.at[1, n]) for n, (_, mid, dst) in enumerate(parts)]
    for read in reads:
        read.start()
    for read, write in zip(reads, writes):
        read.wait()
        write.start()
    for write in writes:
        write.wait()


def shards(tokens, cotangent, expert_ids, probs, w_gate, w_up, w_down):
    any_ = pl.BlockSpec(memory_space=pl.ANY)
    vmem = pl.BlockSpec(memory_space=pltpu.VMEM)
    dma = pltpu.SemaphoreType.DMA
    v = pltpu.VMEM
    gt, gg, gu, gd = pl.pallas_call(
        kernel,
        out_shape=(
            jax.ShapeDtypeStruct((TOK, D), BF16),
            jax.ShapeDtypeStruct((DS, F), BF16),
            jax.ShapeDtypeStruct((DS, F), BF16),
            jax.ShapeDtypeStruct((F, DS), BF16),
        ),
        in_specs=[vmem, vmem] + [any_] * 5,
        out_specs=(any_,) * 4,
        scratch_shapes=[
            v((J, TOK, DS), BF16), v((J, TOK, DS), BF16),
            v((J, DS, 2 * F), BF16), v((J, F, DS), BF16),
            v((J, HALF, DS), BF16), v((HALF, DS), BF16),
            v((J, HALF, DS), BF16), v((HALF, DS), BF16),
            v((J, ROWS, DS), BF16), v((2 * HALF, DS), BF16),
            v((J, ROWS, DS), BF16), v((2 * HALF, DS), BF16),
            v((HALF, TOK), BF16), v((HALF, TOK), BF16),
            v((TOK, HALF), BF16), v((TOK, HALF), BF16),
            v((2, HALF, TOK), F32),
            v((ROWS, 2 * F), F32), v((ROWS, F), F32),
            v((ROWS, 2 * F), BF16), v((3 * F, ROWS), BF16),
            v((J, ROWS, DS), BF16), v((2 * HALF, DS), BF16),
            v((J, HALF, DS), BF16), v((HALF, DS), BF16),
            v((J, HALF, DS), BF16), v((HALF, DS), BF16),
            v((J, HALF, DS), BF16), v((HALF, DS), BF16),
            v((24, 4, UNIT, DS), BF16), v((12, UNIT, DS), BF16), v((16, UNIT, DS), F32),
            v((3 * F, DS), BF16), v((2, DS, F), BF16),
            dma((8,)), dma((23,)), dma((23,)), dma((27,)), dma((27,)),
            dma((24, 4)), dma((24, 4)),
        ],
        compiler_params=pltpu.CompilerParams(
            collective_id=0, has_side_effects=True, vmem_limit_bytes=60 * 2**20
        ),
        cost_estimate=pl.CostEstimate(
            flops=15_000_000_000, bytes_accessed=14_000_000, transcendentals=500_000
        ),
    )(expert_ids.T, probs.T, tokens, cotangent, w_gate[0], w_up[0], w_down[0])
    found = (gt, gg, gu, gd)
    gt, gg, gu, gd = pl.pallas_call(
        write_out,
        out_shape=tuple(jax.ShapeDtypeStruct(a.shape, a.dtype) for a in found),
        in_specs=[any_] * 4,
        out_specs=(any_,) * 4,
        scratch_shapes=[v(a.shape, a.dtype) for a in found] + [dma((2, 7))],
    )(*found)
    return gt, gg[None], gu[None], gd[None]


def solution(mesh):
    in_specs = (
        P(("dp", "expert"), None),
        P(("dp", "expert"), None),
        P(("dp", "expert"), None),
        P(("dp", "expert"), None),
        P("expert", None, None),
        P("expert", None, None),
        P("expert", None, None),
    )
    out_specs = (
        P(("dp", "expert"), None),
        P("expert", "dp", None),
        P("expert", "dp", None),
        P("expert", None, "dp"),
    )
    return jax.shard_map(shards, mesh=mesh, in_specs=in_specs, out_specs=out_specs, check_vma=False)
```

```python
import jax
import jax.numpy as jnp
from jax import lax
from jax.experimental import pallas as pl
from jax.experimental.pallas import tpu as pltpu
from jax.sharding import PartitionSpec as P

D = 4096
F = 384
TOK = 128
N_DP = 8
CHIPS = 16
J = 8
DS = D // J
MAIN = 16
HALF = CHIPS * MAIN
ROWS = 2 * HALF + 64
UNIT = 96
MESH = pl.DeviceIdType.MESH
F32 = jnp.float32
BF16 = jnp.bfloat16
OTHERS = (
    (0, 1), (1, 0), (0, 3), (3, 0), (1, 1), (3, 3), (1, 3), (3, 1),
    (0, 2), (2, 0), (2, 1), (1, 2), (2, 3), (3, 2), (2, 2),
)
X_AT, XE_AT, S_AT, SE_AT, R_AT, RE_AT = 0, 8, 9, 17, 18, 22
RG_AT, RGE_AT = 18, 26
LAG = 2


def mm(a, b):
    return jnp.dot(a, b, preferred_element_type=F32)


def mm_nt(a, b):
    return lax.dot_general(a, b, (((1,), (1,)), ((), ())), preferred_element_type=F32)


def iota(shape, dim):
    return lax.broadcasted_iota(jnp.int32, shape, dim)


def eye(n):
    return (iota((n, n), 0) == iota((n, n), 1)).astype(BF16)


def kernel(
    ids_in, probs_in, tok, cot, wg, wu, wd,
    gt, grads,
    ids, probs, tokb, cotb, w_gu, w_d, xs, xse, ss, sse, X, XE, S, SE,
    pick, pick_e, pick_t, pick_et, scales, pre, gh, ggu, at,
    RG, RGE, RV, RVE, PS, PSE, RT, RTE, ring, begin, psum, gds,
    loc, snd, rcv, sib_s, sib_r, ring_s, ring_r,
):
    z = lax.axis_index("dp")
    e = lax.axis_index("expert")
    k = lax.rem(e, 2)
    c = e // 2
    cy = c // 4
    cx = lax.rem(c, 4)
    sibling = (z, c * 2 + (1 - k))
    z_next = (lax.rem(z + 1, N_DP), e)
    z_prev = (lax.rem(z + N_DP - 1, N_DP), e)
    chip_of = [lax.rem(cy + dy, 4) * 4 + lax.rem(cx + dx, 4) for dy, dx in OTHERS]

    barrier = pltpu.get_barrier_semaphore()
    for dev in (z_next, z_prev):
        pl.semaphore_signal(barrier, inc=1, device_id=dev, device_id_type=MESH)
    for chip in chip_of:
        pl.semaphore_signal(barrier, inc=1, device_id=(z, chip * 2 + k), device_id_type=MESH)
    pl.semaphore_signal(barrier, inc=1, device_id=sibling, device_id_type=MESH)
    pltpu.make_async_copy(ids_in, ids, loc.at[6]).start()
    pltpu.make_async_copy(probs_in, probs, loc.at[7]).start()
    for j in range(J):
        pltpu.make_async_copy(tok.at[:, pl.ds(j * DS, DS)], tokb.at[j], loc.at[0]).start()

    def wait_bytes(ref, sem):
        pltpu.make_async_copy(ref, ref, sem).wait()

    wait_bytes(ids, loc.at[6])
    wait_bytes(probs, loc.at[7])
    id0, id1 = ids[0:1, :], ids[1:2, :]
    p0, p1 = probs[0:1, :], probs[1:2, :]
    row = iota((HALF, TOK), 0)
    expert, slot = row // MAIN, lax.rem(row, MAIN)
    named0, named1 = id0 == expert, id1 == expert
    named = named0 | named1
    before = (iota((TOK, TOK), 0) < iota((TOK, TOK), 1)).astype(BF16)
    rank = mm(named.astype(F32).astype(BF16), before).astype(jnp.int32)
    main = named & (rank == slot)
    extra = named & (rank == MAIN + lax.rem(slot, 2))
    pick[...] = main.astype(F32).astype(BF16)
    pick_e[...] = extra.astype(F32).astype(BF16)

    def scale_of(picked):
        each = jnp.where(picked & named0, p0, 0.0) + jnp.where(picked & named1, p1, 0.0)
        return jnp.broadcast_to(jnp.sum(each, axis=1, keepdims=True), (HALF, TOK))

    scales[0] = scale_of(main)
    scales[1] = scale_of(extra)
    part = lax.rem(iota((HALF, TOK), 0), MAIN) // 2

    def extras_of(source):
        def add(j, total):
            chosen = jnp.where(part == j, pick_e[...].astype(F32), 0.0).astype(BF16)
            return total + mm(chosen, source[j])
        return lax.fori_loop(0, J, add, jnp.zeros((HALF, DS), F32))

    def blk(i):
        return pl.ds(pl.multiple_of(i * MAIN, MAIN), MAIN)

    def home(i):
        return pl.ds(pl.multiple_of(k * HALF + i * MAIN, MAIN), MAIN)

    mine = pl.ds(pl.multiple_of(k * HALF, HALF), HALF)
    theirs = pl.ds(pl.multiple_of((1 - k) * HALF, HALF), HALF)

    def send_all(src_of, dst, at_sem):
        for chip in chip_of:
            pltpu.make_async_remote_copy(
                src_ref=src_of(chip), dst_ref=dst,
                send_sem=snd.at[at_sem], recv_sem=rcv.at[at_sem],
                device_id=(z, chip * 2 + k), device_id_type=MESH,
            ).start()
        pltpu.make_async_copy(src_of(c), dst, rcv.at[at_sem]).start()

    def to_sibling(src, dst, at_sem):
        return pltpu.make_async_remote_copy(
            src_ref=src, dst_ref=dst, send_sem=sib_s.at[at_sem], recv_sem=sib_r.at[at_sem],
            device_id=sibling, device_id_type=MESH,
        )

    wait_bytes(tokb, loc.at[0])

    def send_tok(j):
        send_all(lambda i: xs.at[j, blk(i), :], X.at[j, home(c), :], X_AT + j)

    xs[0] = mm(pick[...], tokb[0]).astype(BF16)
    pl.semaphore_wait(barrier, len(OTHERS) + 3)
    send_tok(0)
    xse[...] = extras_of(tokb).astype(BF16)
    send_all(lambda i: xse.at[blk(i), :], XE.at[home(c), :], XE_AT)

    @pl.loop(1, J)
    def _(j):
        xs[j] = mm(pick[...], tokb[j]).astype(BF16)
        send_tok(j)

    for j in range(J):
        pltpu.make_async_copy(cot.at[:, pl.ds(j * DS, DS)], cotb.at[j], loc.at[1]).start()
    for j in range(J):
        rows = pl.ds(j * DS, DS)
        pltpu.make_async_copy(wg.at[rows, :], w_gu.at[j, :, pl.ds(0, F)], loc.at[2]).start()
        pltpu.make_async_copy(wu.at[rows, :], w_gu.at[j, :, pl.ds(F, F)], loc.at[2]).start()
    for j in range(J):
        pltpu.make_async_copy(wd.at[:, pl.ds(j * DS, DS)], w_d.at[j], loc.at[3]).start()

    wait_bytes(cotb, loc.at[1])
    sse[...] = (extras_of(cotb) * scales[1][:, 0:1]).astype(BF16)
    pick_t[...] = mm_nt(eye(TOK), pick[...]).astype(BF16)
    pick_et[...] = mm_nt(eye(TOK), pick_e[...]).astype(BF16)
    pre[...] = jnp.zeros_like(pre)
    gh[...] = jnp.zeros_like(gh)

    def place(t, up):
        return lax.rem(z + 12 - t, N_DP) if up else lax.rem(z + 4 + t, N_DP)

    def order(i):
        odd = lax.rem(i, 2)
        return place((i + 1) // 2, True) * odd + place(i // 2, False) * (1 - odd)

    def send_cot(i):
        o = order(i)
        ss[o] = (mm(pick[...], cotb[o]) * scales[0][:, 0:1]).astype(BF16)
        send_all(lambda n: ss.at[o, blk(n), :], S.at[o, home(c), :], S_AT + i)

    def unpack(j):
        r, col = iota((64, 2 * HALF), 0), iota((64, 2 * HALF), 1)
        return (col == (r // 2) * MAIN + 2 * j + lax.rem(r, 2)).astype(F32).astype(BF16)

    def unpack_t(j):
        r, col = iota((2 * HALF, 64), 1), iota((2 * HALF, 64), 0)
        return (col == (r // 2) * MAIN + 2 * j + lax.rem(r, 2)).astype(F32).astype(BF16)

    tail = pl.ds(2 * HALF, 64)

    wait_bytes(XE.at[pl.ds(0, HALF), :], rcv.at[XE_AT])
    fwd_xe = to_sibling(XE.at[mine, :], XE.at[mine, :], XE_AT)
    fwd_xe.start()
    fwd_xe.wait_recv()

    @pl.loop(0, J)
    def _(j):
        X[j, tail, :] = mm(unpack(j), XE[...]).astype(BF16)

    send_all(lambda i: sse.at[blk(i), :], SE.at[home(c), :], SE_AT)
    wait_bytes(w_gu, loc.at[2])

    @pl.loop(0, J)
    def _(j):
        wait_bytes(X.at[j, pl.ds(0, HALF), :], rcv.at[X_AT + j])
        fwd = to_sibling(X.at[j, mine, :], X.at[j, mine, :], X_AT + j)
        fwd.start()

        @pl.when(j >= LAG)
        def _():
            send_cot(j - LAG)

        fwd.wait_recv()
        pre[...] += mm(X[j], w_gu[j])

    def store_t(first, value):
        at[pl.ds(first, F), :] = mm_nt(eye(F), value).astype(BF16)

    gate, up = pre[:, 0:F], pre[:, F:2 * F]
    store_t(2 * F, (gate * jax.nn.sigmoid(gate) * up).astype(BF16))

    def pass_on(v, t, src, up):
        pltpu.make_async_remote_copy(
            src_ref=src, dst_ref=ring.at[v, t],
            send_sem=ring_s.at[v, t], recv_sem=ring_r.at[v, t],
            device_id=z_next if up else z_prev, device_id_type=MESH,
        ).start()

    down, gate_up = (0, 4, 2 * F), (4, 8, 0)

    def begin_chains(group, source):
        u0, n, first = group
        terms = mm(at[pl.ds(first, n * UNIT), :], source[place(0, False)])
        for m in range(n):
            begin[u0 + m] = terms[m * UNIT:(m + 1) * UNIT].astype(BF16)

        @pl.loop(0, n // 2)
        def _(m):
            pass_on(u0 + m, 0, begin.at[u0 + m], False)
            pass_on(12 + u0 + n // 2 + m, 0, begin.at[u0 + n // 2 + m], True)

    def terms_of(group, t, up, source):
        u0, n, first = group
        terms = mm(at[pl.ds(first, n * UNIT), :], source[place(t, up)])
        for m in range(n):
            psum[up * 8 + m] = terms[m * UNIT:(m + 1) * UNIT]

    def hop(group, m, t, up, joins):
        v = up * 12 + group[0] + m
        slot_ref = ring.at[v, t - 1]
        if joins:
            wait_bytes(slot_ref, ring_r.at[v, t - 1])
            slot_ref[...] = (psum[up * 8 + m] + slot_ref[...].astype(F32)).astype(BF16)
        else:
            slot_ref[...] = psum[up * 8 + m].astype(BF16)
        pass_on(v, t, slot_ref, up)

    def hops(group, t, half, ups):
        n = group[1]

        @pl.loop(0, n // 2)
        def _(m):
            joins = t > 1 or half == 1
            for up in ups:
                upper = (half == 0) != bool(up)
                hop(group, m + (n // 2 if upper else 0), t, up, joins)

    def end_chains(group, source):
        u0, n, first = group
        terms_of(group, 4, 0, source)

        def end(m):
            for up in range(2):
                wait_bytes(ring.at[up * 12 + u0 + m, 3], ring_r.at[up * 12 + u0 + m, 3])
            came = ring[u0 + m, 3].astype(F32) + ring[12 + u0 + m, 3].astype(F32)
            rows = pl.ds(pl.multiple_of(first + m * UNIT, UNIT), UNIT)
            gds[rows, :] = (psum[m] + came).astype(BF16)

        @pl.loop(0, n // 2)
        def _(m):
            end(m)
            end(n // 2 + m)

    def forward(i):
        o = order(i)
        wait_bytes(S.at[o, pl.ds(0, HALF), :], rcv.at[S_AT + i])
        to_sibling(S.at[o, mine, :], S.at[o, mine, :], S_AT + i).start()

    def fill_tail(i):
        o = order(i)
        S[o, tail, :] = mm(unpack(o), SE[...]).astype(BF16)

    def here(i):
        o = order(i)
        to_sibling(S.at[o, mine, :], S.at[o, mine, :], S_AT + i).wait_recv()

    def grad_hidden(i):
        o = order(i)
        gh[...] += mm_nt(S[o], w_d[o])

    def down_step(t, up):
        terms_of(down, t, up, S)
        hops(down, t, 0, (up,))
        hops(down, t, 1, (up,))

    wait_bytes(SE.at[pl.ds(0, HALF), :], rcv.at[SE_AT])
    fwd_se = to_sibling(SE.at[mine, :], SE.at[mine, :], SE_AT)
    fwd_se.start()
    forward(0)
    fwd_se.wait_recv()
    fill_tail(0)
    here(0)
    begin_chains(down, S)

    @pl.loop(J - LAG, J)
    def _(i):
        send_cot(i)

    wait_bytes(w_d, loc.at[3])
    for i in range(1, 7):
        forward(i)
        fill_tail(i)
        grad_hidden(i - 1)
        here(i)
        if i == 6:
            forward(7)
            fill_tail(7)
        down_step((i + 1) // 2, i % 2)
    grad_hidden(6)
    here(7)
    grad_hidden(7)

    gate, up, grad = pre[:, 0:F], pre[:, F:2 * F], gh[...]
    sig = jax.nn.sigmoid(gate)
    ggate = (grad * up * sig * (1.0 + gate * (1.0 - sig))).astype(BF16)
    gup = (grad * gate * sig).astype(BF16)
    ggu[:, 0:F] = ggate
    ggu[:, F:2 * F] = gup
    store_t(0, ggate)
    store_t(F, gup)

    def row_grad(j):
        RG[j] = mm_nt(ggu[...], w_gu[j]).astype(BF16)
        to_sibling(RG.at[j, theirs, :], RV.at[j], RG_AT + j).start()

    def pair_grad(q):
        for n in range(2):
            j = 2 * q + n
            to_sibling(RG.at[j, theirs, :], RV.at[j], RG_AT + j).wait_recv()
            PS[j] = (RG[j, mine, :].astype(F32) + RV[j].astype(F32)).astype(BF16)
        two = pl.ds(2 * q, 2)
        send_all(lambda i: PS.at[two, blk(i), :], RT.at[two, blk(c), :], R_AT + q)

    def row_grad_extras():
        def add(j, total):
            return total + mm(unpack_t(j), RG[j, tail, :])
        RGE[...] = lax.fori_loop(0, J, add, jnp.zeros((2 * HALF, DS), F32)).astype(BF16)
        to_sibling(RGE.at[theirs, :], RVE, RGE_AT).start()

    def pair_grad_extras():
        to_sibling(RGE.at[theirs, :], RVE, RGE_AT).wait_recv()
        PSE[...] = (RGE[mine, :].astype(F32) + RVE[...].astype(F32)).astype(BF16)
        send_all(lambda i: PSE.at[blk(i), :], RTE.at[blk(c), :], RE_AT)

    part_col = lax.rem(iota((TOK, HALF), 1), MAIN) // 2

    def token_grad(q):
        two = pl.ds(2 * q, 2)
        wait_bytes(RT.at[two], rcv.at[R_AT + q])
        for n in range(2):
            j = 2 * q + n
            chosen = jnp.where(part_col == j, pick_et[...].astype(F32), 0.0).astype(BF16)
            tokb[j] = (mm(pick_t[...], RT[j]) + mm(chosen, RTE[...])).astype(BF16)
            cols = pl.ds(pl.multiple_of(j * DS, DS), DS)
            pltpu.make_async_copy(tokb.at[j], gt.at[:, cols], loc.at[4]).start()

    def several(first, last, what):
        @pl.loop(first, last)
        def _(n):
            what(n)

    begin_chains(gate_up, X)
    several(0, 4, row_grad)
    for t in range(1, 4):
        terms_of(gate_up, t, 1, X)
        terms_of(gate_up, t, 0, X)
        hops(gate_up, t, 0, (1, 0))
        if t == 1:
            several(4, 8, row_grad)
            pair_grad(0)
            pair_grad(1)
        if t == 2:
            pair_grad_extras()
        hops(gate_up, t, 1, (1, 0))
        if t == 1:
            several(2, 4, pair_grad)
            row_grad_extras()
    end_chains(down, S)
    def out(first, rows):
        rows = pl.ds(first, rows)
        pltpu.make_async_copy(gds.at[rows, :], grads.at[rows, :], loc.at[5]).start()

    out(2 * F, F)
    wait_bytes(RTE, rcv.at[RE_AT])
    several(0, 4, token_grad)

    def sent(ref, sem):
        wait_bytes(ref, sem)

    less = HALF - MAIN
    for q in range(4):
        two = pl.ds(2 * q, 2)
        sent(PS.at[two, pl.ds(0, less), :], snd.at[R_AT + q])
    for i in range(J):
        sent(xs.at[i, pl.ds(0, less), :], snd.at[X_AT + i])
        sent(ss.at[i, pl.ds(0, less), :], snd.at[S_AT + i])
        sent(xs.at[i], sib_s.at[X_AT + i])
        sent(ss.at[i], sib_s.at[S_AT + i])
        sent(RV.at[i], sib_s.at[RG_AT + i])
    for at_sem in (XE_AT, SE_AT, RE_AT):
        sent(xse.at[pl.ds(0, less), :], snd.at[at_sem])
    for at_sem in (XE_AT, SE_AT, RGE_AT):
        sent(xse, sib_s.at[at_sem])

    for u0, n, _ in (down, gate_up):
        for m in range(n // 2):
            sent(begin.at[0], ring_s.at[u0 + m, 0])
            sent(begin.at[0], ring_s.at[12 + u0 + n // 2 + m, 0])

    @pl.loop(0, 24)
    def _(v):
        for t in range(1, 3):
            sent(ring.at[v, t], ring_s.at[v, t])

    wait_bytes(tokb, loc.at[4])
    end_chains(gate_up, X)
    out(0, 2 * F)

    @pl.loop(0, 24)
    def _(v):
        sent(ring.at[v, 3], ring_s.at[v, 3])

    wait_bytes(gds, loc.at[5])


def write_out(gt, grads, gt_out, gg_out, gu_out, gd_out, gt_v, grads_v, turned, sem):
    parts = [
        pltpu.make_async_copy(grads.at[pl.ds(n * F, F), :], grads_v.at[pl.ds(n * F, F), :], sem.at[n])
        for n in range(3)
    ]
    rows = [pl.ds(32 * n, 32) for n in range(4)]
    tokens = [pltpu.make_async_copy(gt.at[r, :], gt_v.at[r, :], sem.at[3 + n]) for n, r in enumerate(rows)]
    for read in parts + tokens:
        read.start()
    writes = []

    def write(src, dst):
        writes.append(pltpu.make_async_copy(src, dst, sem.at[7 + len(writes)]))
        writes[-1].start()

    for n, dst in enumerate((gg_out, gu_out)):
        parts[n].wait()
        turned[n] = mm_nt(eye(DS), grads_v[n * F:(n + 1) * F, :]).astype(BF16)
        write(turned.at[n], dst)
    parts[2].wait()
    write(grads_v.at[pl.ds(2 * F, F), :], gd_out)
    for n, r in enumerate(rows):
        tokens[n].wait()
        write(gt_v.at[r, :], gt_out.at[r, :])
    for copy in writes:
        copy.wait()


def shards(tokens, cotangent, expert_ids, probs, w_gate, w_up, w_down):
    any_ = pl.BlockSpec(memory_space=pl.ANY)
    dma = pltpu.SemaphoreType.DMA
    v = pltpu.VMEM
    gt, grads = pl.pallas_call(
        kernel,
        out_shape=(
            jax.ShapeDtypeStruct((TOK, D), BF16),
            jax.ShapeDtypeStruct((3 * F, DS), BF16),
        ),
        in_specs=[any_] * 7,
        out_specs=(any_,) * 2,
        scratch_shapes=[
            v((2, TOK), jnp.int32), v((2, TOK), F32),
            v((J, TOK, DS), BF16), v((J, TOK, DS), BF16),
            v((J, DS, 2 * F), BF16), v((J, F, DS), BF16),
            v((J, HALF, DS), BF16), v((HALF, DS), BF16),
            v((J, HALF, DS), BF16), v((HALF, DS), BF16),
            v((J, ROWS, DS), BF16), v((2 * HALF, DS), BF16),
            v((J, ROWS, DS), BF16), v((2 * HALF, DS), BF16),
            v((HALF, TOK), BF16), v((HALF, TOK), BF16),
            v((TOK, HALF), BF16), v((TOK, HALF), BF16),
            v((2, HALF, TOK), F32),
            v((ROWS, 2 * F), F32), v((ROWS, F), F32),
            v((ROWS, 2 * F), BF16), v((3 * F, ROWS), BF16),
            v((J, ROWS, DS), BF16), v((2 * HALF, DS), BF16),
            v((J, HALF, DS), BF16), v((HALF, DS), BF16),
            v((J, HALF, DS), BF16), v((HALF, DS), BF16),
            v((J, HALF, DS), BF16), v((HALF, DS), BF16),
            v((24, 4, UNIT, DS), BF16), v((12, UNIT, DS), BF16), v((16, UNIT, DS), F32),
            v((3 * F, DS), BF16),
            dma((8,)), dma((23,)), dma((23,)), dma((27,)), dma((27,)),
            dma((24, 4)), dma((24, 4)),
        ],
        compiler_params=pltpu.CompilerParams(
            collective_id=0, has_side_effects=True, vmem_limit_bytes=60 * 2**20
        ),
        cost_estimate=pl.CostEstimate(
            flops=15_000_000_000, bytes_accessed=14_000_000, transcendentals=500_000
        ),
    )(expert_ids.T, probs.T, tokens, cotangent, w_gate[0], w_up[0], w_down[0])
    gt, gg, gu, gd = pl.pallas_call(
        write_out,
        out_shape=(
            jax.ShapeDtypeStruct((TOK, D), BF16),
            jax.ShapeDtypeStruct((DS, F), BF16),
            jax.ShapeDtypeStruct((DS, F), BF16),
            jax.ShapeDtypeStruct((F, DS), BF16),
        ),
        in_specs=[any_] * 2,
        out_specs=(any_,) * 4,
        scratch_shapes=[v((TOK, D), BF16), v((3 * F, DS), BF16), v((2, DS, F), BF16), dma((14,))],
    )(gt, grads)
    return gt, gg[None], gu[None], gd[None]


def solution(mesh):
    in_specs = (
        P(("dp", "expert"), None),
        P(("dp", "expert"), None),
        P(("dp", "expert"), None),
        P(("dp", "expert"), None),
        P("expert", None, None),
        P("expert", None, None),
        P("expert", None, None),
    )
    out_specs = (
        P(("dp", "expert"), None),
        P("expert", "dp", None),
        P("expert", "dp", None),
        P("expert", None, "dp"),
    )
    return jax.shard_map(shards, mesh=mesh, in_specs=in_specs, out_specs=out_specs, check_vma=False)
```

```python
import jax
import jax.numpy as jnp
from jax import lax
from jax.experimental import pallas as pl
from jax.experimental.pallas import tpu as pltpu
from jax.sharding import PartitionSpec as P

D = 4096
F = 384
TOK = 128
N_DP = 8
CHIPS = 16
J = 8
DS = D // J
MAIN = 16
HALF = CHIPS * MAIN
ROWS = 2 * HALF + 64
UNIT = 96
MESH = pl.DeviceIdType.MESH
F32 = jnp.float32
BF16 = jnp.bfloat16
OTHERS = (
    (0, 1), (1, 0), (0, 3), (3, 0), (1, 1), (3, 3), (1, 3), (3, 1),
    (0, 2), (2, 0), (2, 1), (1, 2), (2, 3), (3, 2), (2, 2),
)
X_AT, XE_AT, S_AT, SE_AT, R_AT, RE_AT = 0, 8, 9, 17, 18, 22
RG_AT, RGE_AT = 18, 26
LAG = 2


def mm(a, b):
    return jnp.dot(a, b, preferred_element_type=F32)


def mm_nt(a, b):
    return lax.dot_general(a, b, (((1,), (1,)), ((), ())), preferred_element_type=F32)


def iota(shape, dim):
    return lax.broadcasted_iota(jnp.int32, shape, dim)


def eye(n):
    return (iota((n, n), 0) == iota((n, n), 1)).astype(BF16)


def kernel(
    ids_in, probs_in, tok, cot, wg, wu, wd,
    gt, grads,
    ids, probs, tokb, cotb, w_gu, w_d, xs, xse, ss, sse, X, XE, S, SE,
    pick, pick_e, pick_t, pick_et, scales, pre, gh, ggu, at,
    RG, RGE, RV, RVE, PS, PSE, RT, RTE, ring, begin, psum, gds,
    loc, snd, rcv, sib_s, sib_r, ring_s, ring_r,
):
    z = lax.axis_index("dp")
    e = lax.axis_index("expert")
    k = lax.rem(e, 2)
    c = e // 2
    cy = c // 4
    cx = lax.rem(c, 4)
    sibling = (z, c * 2 + (1 - k))
    z_next = (lax.rem(z + 1, N_DP), e)
    z_prev = (lax.rem(z + N_DP - 1, N_DP), e)
    chip_of = [lax.rem(cy + dy, 4) * 4 + lax.rem(cx + dx, 4) for dy, dx in OTHERS]

    barrier = pltpu.get_barrier_semaphore()
    for dev in (z_next, z_prev):
        pl.semaphore_signal(barrier, inc=1, device_id=dev, device_id_type=MESH)
    for chip in chip_of:
        pl.semaphore_signal(barrier, inc=1, device_id=(z, chip * 2 + k), device_id_type=MESH)
    pl.semaphore_signal(barrier, inc=1, device_id=sibling, device_id_type=MESH)
    pltpu.make_async_copy(ids_in, ids, loc.at[6]).start()
    pltpu.make_async_copy(probs_in, probs, loc.at[7]).start()
    for j in range(J):
        pltpu.make_async_copy(tok.at[:, pl.ds(j * DS, DS)], tokb.at[j], loc.at[0]).start()

    def wait_bytes(ref, sem):
        pltpu.make_async_copy(ref, ref, sem).wait()

    wait_bytes(ids, loc.at[6])
    wait_bytes(probs, loc.at[7])
    id0, id1 = ids[0:1, :], ids[1:2, :]
    p0, p1 = probs[0:1, :], probs[1:2, :]
    row = iota((HALF, TOK), 0)
    expert, slot = row // MAIN, lax.rem(row, MAIN)
    named0, named1 = id0 == expert, id1 == expert
    named = named0 | named1
    before = (iota((TOK, TOK), 0) < iota((TOK, TOK), 1)).astype(BF16)
    rank = mm(named.astype(F32).astype(BF16), before).astype(jnp.int32)
    main = named & (rank == slot)
    extra = named & (rank == MAIN + lax.rem(slot, 2))
    pick[...] = main.astype(F32).astype(BF16)
    pick_e[...] = extra.astype(F32).astype(BF16)

    def scale_of(picked):
        each = jnp.where(picked & named0, p0, 0.0) + jnp.where(picked & named1, p1, 0.0)
        return jnp.broadcast_to(jnp.sum(each, axis=1, keepdims=True), (HALF, TOK))

    scales[0] = scale_of(main)
    scales[1] = scale_of(extra)
    part = lax.rem(iota((HALF, TOK), 0), MAIN) // 2

    def extras_of(source):
        def add(j, total):
            chosen = jnp.where(part == j, pick_e[...].astype(F32), 0.0).astype(BF16)
            return total + mm(chosen, source[j])
        return lax.fori_loop(0, J, add, jnp.zeros((HALF, DS), F32))

    def blk(i):
        return pl.ds(pl.multiple_of(i * MAIN, MAIN), MAIN)

    def home(i):
        return pl.ds(pl.multiple_of(k * HALF + i * MAIN, MAIN), MAIN)

    mine = pl.ds(pl.multiple_of(k * HALF, HALF), HALF)
    theirs = pl.ds(pl.multiple_of((1 - k) * HALF, HALF), HALF)

    def send_all(src_of, dst, at_sem):
        for chip in chip_of:
            pltpu.make_async_remote_copy(
                src_ref=src_of(chip), dst_ref=dst,
                send_sem=snd.at[at_sem], recv_sem=rcv.at[at_sem],
                device_id=(z, chip * 2 + k), device_id_type=MESH,
            ).start()
        pltpu.make_async_copy(src_of(c), dst, rcv.at[at_sem]).start()

    def to_sibling(src, dst, at_sem):
        return pltpu.make_async_remote_copy(
            src_ref=src, dst_ref=dst, send_sem=sib_s.at[at_sem], recv_sem=sib_r.at[at_sem],
            device_id=sibling, device_id_type=MESH,
        )

    wait_bytes(tokb, loc.at[0])

    def send_tok(j):
        send_all(lambda i: xs.at[j, blk(i), :], X.at[j, home(c), :], X_AT + j)

    xs[0] = mm(pick[...], tokb[0]).astype(BF16)
    pl.semaphore_wait(barrier, len(OTHERS) + 3)
    send_tok(0)
    xse[...] = extras_of(tokb).astype(BF16)
    send_all(lambda i: xse.at[blk(i), :], XE.at[home(c), :], XE_AT)

    @pl.loop(1, J)
    def _(j):
        xs[j] = mm(pick[...], tokb[j]).astype(BF16)
        send_tok(j)

    for j in range(J):
        pltpu.make_async_copy(cot.at[:, pl.ds(j * DS, DS)], cotb.at[j], loc.at[1]).start()
    for j in range(J):
        rows = pl.ds(j * DS, DS)
        pltpu.make_async_copy(wg.at[rows, :], w_gu.at[j, :, pl.ds(0, F)], loc.at[2]).start()
        pltpu.make_async_copy(wu.at[rows, :], w_gu.at[j, :, pl.ds(F, F)], loc.at[2]).start()
    for j in range(J):
        pltpu.make_async_copy(wd.at[:, pl.ds(j * DS, DS)], w_d.at[j], loc.at[3]).start()

    wait_bytes(cotb, loc.at[1])
    sse[...] = (extras_of(cotb) * scales[1][:, 0:1]).astype(BF16)
    pick_t[...] = mm_nt(eye(TOK), pick[...]).astype(BF16)
    pick_et[...] = mm_nt(eye(TOK), pick_e[...]).astype(BF16)
    pre[...] = jnp.zeros_like(pre)
    gh[...] = jnp.zeros_like(gh)

    def place(t, up):
        return lax.rem(z + 12 - t, N_DP) if up else lax.rem(z + 4 + t, N_DP)

    def order(i):
        odd = lax.rem(i, 2)
        return place((i + 1) // 2, True) * odd + place(i // 2, False) * (1 - odd)

    def send_cot(i):
        o = order(i)
        ss[o] = (mm(pick[...], cotb[o]) * scales[0][:, 0:1]).astype(BF16)
        send_all(lambda n: ss.at[o, blk(n), :], S.at[o, home(c), :], S_AT + i)

    def unpack(j):
        r, col = iota((64, 2 * HALF), 0), iota((64, 2 * HALF), 1)
        return (col == (r // 2) * MAIN + 2 * j + lax.rem(r, 2)).astype(F32).astype(BF16)

    def unpack_t(j):
        r, col = iota((2 * HALF, 64), 1), iota((2 * HALF, 64), 0)
        return (col == (r // 2) * MAIN + 2 * j + lax.rem(r, 2)).astype(F32).astype(BF16)

    tail = pl.ds(2 * HALF, 64)

    wait_bytes(XE.at[pl.ds(0, HALF), :], rcv.at[XE_AT])
    fwd_xe = to_sibling(XE.at[mine, :], XE.at[mine, :], XE_AT)
    fwd_xe.start()
    fwd_xe.wait_recv()

    @pl.loop(0, J)
    def _(j):
        X[j, tail, :] = mm(unpack(j), XE[...]).astype(BF16)

    send_all(lambda i: sse.at[blk(i), :], SE.at[home(c), :], SE_AT)
    wait_bytes(w_gu, loc.at[2])

    @pl.loop(0, J)
    def _(j):
        wait_bytes(X.at[j, pl.ds(0, HALF), :], rcv.at[X_AT + j])
        fwd = to_sibling(X.at[j, mine, :], X.at[j, mine, :], X_AT + j)
        fwd.start()

        @pl.when(j >= LAG)
        def _():
            send_cot(j - LAG)

        fwd.wait_recv()
        pre[...] += mm(X[j], w_gu[j])

    def store_t(first, value):
        at[pl.ds(first, F), :] = mm_nt(eye(F), value).astype(BF16)

    gate, up = pre[:, 0:F], pre[:, F:2 * F]
    store_t(2 * F, (gate * jax.nn.sigmoid(gate) * up).astype(BF16))

    def several(first, last, what):
        @pl.loop(first, last)
        def _(n):
            what(n)

    def pass_on(v, t, src, up):
        pltpu.make_async_remote_copy(
            src_ref=src, dst_ref=ring.at[v, t],
            send_sem=ring_s.at[v, t], recv_sem=ring_r.at[v, t],
            device_id=z_next if up else z_prev, device_id_type=MESH,
        ).start()

    down, gate_up = (0, 4, 2 * F, 3), (4, 8, 0, 3)

    def begin_chains(group, source):
        u0, n, first, lo = group
        terms = mm(at[pl.ds(first, n * UNIT), :], source[place(0, False)])
        for m in range(n):
            begin[u0 + m] = terms[m * UNIT:(m + 1) * UNIT].astype(BF16)

        @pl.loop(0, lo)
        def _(m):
            pass_on(u0 + m, 0, begin.at[u0 + m], False)

        @pl.loop(lo, n)
        def _(m):
            pass_on(12 + u0 + m, 0, begin.at[u0 + m], True)

    def terms_of(group, t, up, source):
        u0, n, first, lo = group
        terms = mm(at[pl.ds(first, n * UNIT), :], source[place(t, up)])
        for m in range(n):
            psum[up * 8 + m] = terms[m * UNIT:(m + 1) * UNIT]

    def hop(group, m, t, up, joins):
        v = up * 12 + group[0] + m
        slot_ref = ring.at[v, t - 1]
        if joins:
            wait_bytes(slot_ref, ring_r.at[v, t - 1])
            slot_ref[...] = (psum[up * 8 + m] + slot_ref[...].astype(F32)).astype(BF16)
        else:
            slot_ref[...] = psum[up * 8 + m].astype(BF16)
        pass_on(v, t, slot_ref, up)

    def hops(group, t, half, ups):
        _, n, _, lo = group
        places = (half * n // 2, (half + 1) * n // 2)
        if t == 1:
            for i in range(*places):
                for up in ups:
                    m = i if up else (i + lo) % n
                    hop(group, m, t, up, (m >= lo) == bool(up))
            return

        @pl.loop(*places)
        def _(i):
            for up in ups:
                hop(group, i if up else lax.rem(i + lo, n), t, up, True)

    def end_chains(group, source):
        u0, n, first, lo = group
        terms_of(group, 4, 0, source)

        def end(m):
            for up in range(2):
                wait_bytes(ring.at[up * 12 + u0 + m, 3], ring_r.at[up * 12 + u0 + m, 3])
            came = ring[u0 + m, 3].astype(F32) + ring[12 + u0 + m, 3].astype(F32)
            rows = pl.ds(pl.multiple_of(first + m * UNIT, UNIT), UNIT)
            gds[rows, :] = (psum[m] + came).astype(BF16)

        if n < 2 * lo:
            several(0, n, end)
            return
        several(lo, n - lo, end)

        @pl.loop(0, lo)
        def _(m):
            end(m)
            end(n - lo + m)

    def forward(i):
        o = order(i)
        wait_bytes(S.at[o, pl.ds(0, HALF), :], rcv.at[S_AT + i])
        to_sibling(S.at[o, mine, :], S.at[o, mine, :], S_AT + i).start()

    def fill_tail(i):
        o = order(i)
        S[o, tail, :] = mm(unpack(o), SE[...]).astype(BF16)

    def here(i):
        o = order(i)
        to_sibling(S.at[o, mine, :], S.at[o, mine, :], S_AT + i).wait_recv()

    def grad_hidden(i):
        o = order(i)
        gh[...] += mm_nt(S[o], w_d[o])

    def down_step(t, up):
        terms_of(down, t, up, S)
        hops(down, t, 0, (up,))
        hops(down, t, 1, (up,))

    wait_bytes(SE.at[pl.ds(0, HALF), :], rcv.at[SE_AT])
    fwd_se = to_sibling(SE.at[mine, :], SE.at[mine, :], SE_AT)
    fwd_se.start()
    forward(0)
    fwd_se.wait_recv()
    fill_tail(0)
    here(0)
    begin_chains(down, S)

    @pl.loop(J - LAG, J)
    def _(i):
        send_cot(i)

    wait_bytes(w_d, loc.at[3])
    for i in range(1, 7):
        forward(i)
        fill_tail(i)
        grad_hidden(i - 1)
        here(i)
        if i == 6:
            forward(7)
            fill_tail(7)
        down_step((i + 1) // 2, i % 2)
    grad_hidden(6)
    here(7)
    grad_hidden(7)

    gate, up, grad = pre[:, 0:F], pre[:, F:2 * F], gh[...]
    sig = jax.nn.sigmoid(gate)
    ggate = (grad * up * sig * (1.0 + gate * (1.0 - sig))).astype(BF16)
    gup = (grad * gate * sig).astype(BF16)
    ggu[:, 0:F] = ggate
    ggu[:, F:2 * F] = gup
    store_t(0, ggate)
    store_t(F, gup)

    def row_grad(j):
        RG[j] = mm_nt(ggu[...], w_gu[j]).astype(BF16)
        to_sibling(RG.at[j, theirs, :], RV.at[j], RG_AT + j).start()

    def pair_grad(q):
        for n in range(2):
            j = 2 * q + n
            to_sibling(RG.at[j, theirs, :], RV.at[j], RG_AT + j).wait_recv()
            PS[j] = (RG[j, mine, :].astype(F32) + RV[j].astype(F32)).astype(BF16)
        two = pl.ds(2 * q, 2)
        send_all(lambda i: PS.at[two, blk(i), :], RT.at[two, blk(c), :], R_AT + q)

    def row_grad_extras():
        def add(j, total):
            return total + mm(unpack_t(j), RG[j, tail, :])
        RGE[...] = lax.fori_loop(0, J, add, jnp.zeros((2 * HALF, DS), F32)).astype(BF16)
        to_sibling(RGE.at[theirs, :], RVE, RGE_AT).start()

    def pair_grad_extras():
        to_sibling(RGE.at[theirs, :], RVE, RGE_AT).wait_recv()
        PSE[...] = (RGE[mine, :].astype(F32) + RVE[...].astype(F32)).astype(BF16)
        send_all(lambda i: PSE.at[blk(i), :], RTE.at[blk(c), :], RE_AT)

    part_col = lax.rem(iota((TOK, HALF), 1), MAIN) // 2

    def token_grad(q):
        two = pl.ds(2 * q, 2)
        wait_bytes(RT.at[two], rcv.at[R_AT + q])
        for n in range(2):
            j = 2 * q + n
            chosen = jnp.where(part_col == j, pick_et[...].astype(F32), 0.0).astype(BF16)
            tokb[j] = (mm(pick_t[...], RT[j]) + mm(chosen, RTE[...])).astype(BF16)
            cols = pl.ds(pl.multiple_of(j * DS, DS), DS)
            pltpu.make_async_copy(tokb.at[j], gt.at[:, cols], loc.at[4]).start()

    begin_chains(gate_up, X)
    several(0, 4, row_grad)
    for t in range(1, 4):
        terms_of(gate_up, t, 1, X)
        terms_of(gate_up, t, 0, X)
        hops(gate_up, t, 0, (1, 0))
        if t == 1:
            several(4, 8, row_grad)
            pair_grad(0)
            pair_grad(1)
        if t == 2:
            pair_grad_extras()
        hops(gate_up, t, 1, (1, 0))
        if t == 1:
            several(2, 4, pair_grad)
            row_grad_extras()
    end_chains(down, S)
    def out(first, rows):
        rows = pl.ds(first, rows)
        pltpu.make_async_copy(gds.at[rows, :], grads.at[rows, :], loc.at[5]).start()

    out(2 * F, F)
    wait_bytes(RTE, rcv.at[RE_AT])
    several(0, 4, token_grad)

    def sent(ref, sem):
        wait_bytes(ref, sem)

    less = HALF - MAIN
    for q in range(4):
        two = pl.ds(2 * q, 2)
        sent(PS.at[two, pl.ds(0, less), :], snd.at[R_AT + q])
    for i in range(J):
        sent(xs.at[i, pl.ds(0, less), :], snd.at[X_AT + i])
        sent(ss.at[i, pl.ds(0, less), :], snd.at[S_AT + i])
        sent(xs.at[i], sib_s.at[X_AT + i])
        sent(ss.at[i], sib_s.at[S_AT + i])
        sent(RV.at[i], sib_s.at[RG_AT + i])
    for at_sem in (XE_AT, SE_AT, RE_AT):
        sent(xse.at[pl.ds(0, less), :], snd.at[at_sem])
    for at_sem in (XE_AT, SE_AT, RGE_AT):
        sent(xse, sib_s.at[at_sem])

    for u0, n, _, lo in (down, gate_up):
        for m in range(n):
            sent(begin.at[0], ring_s.at[u0 + m + (0 if m < lo else 12), 0])

    @pl.loop(0, 24)
    def _(v):
        for t in range(1, 3):
            sent(ring.at[v, t], ring_s.at[v, t])

    wait_bytes(tokb, loc.at[4])
    end_chains(gate_up, X)
    out(0, 2 * F)

    @pl.loop(0, 24)
    def _(v):
        sent(ring.at[v, 3], ring_s.at[v, 3])

    wait_bytes(gds, loc.at[5])


def write_out(gt, grads, gt_out, gg_out, gu_out, gd_out, gt_v, grads_v, turned, sem):
    parts = [
        pltpu.make_async_copy(grads.at[pl.ds(n * F, F), :], grads_v.at[pl.ds(n * F, F), :], sem.at[n])
        for n in range(3)
    ]
    rows = [pl.ds(32 * n, 32) for n in range(4)]
    tokens = [pltpu.make_async_copy(gt.at[r, :], gt_v.at[r, :], sem.at[3 + n]) for n, r in enumerate(rows)]
    for read in tokens + parts[::-1]:
        read.start()
    writes = []

    def write(src, dst):
        writes.append(pltpu.make_async_copy(src, dst, sem.at[7 + len(writes)]))
        writes[-1].start()

    for n, r in enumerate(rows):
        tokens[n].wait()
        write(gt_v.at[r, :], gt_out.at[r, :])
    parts[2].wait()
    write(grads_v.at[pl.ds(2 * F, F), :], gd_out)
    for n, dst in enumerate((gg_out, gu_out)):
        parts[n].wait()
        turned[n] = mm_nt(eye(DS), grads_v[n * F:(n + 1) * F, :]).astype(BF16)
        write(turned.at[n], dst)
    for copy in writes:
        copy.wait()


def shards(tokens, cotangent, expert_ids, probs, w_gate, w_up, w_down):
    any_ = pl.BlockSpec(memory_space=pl.ANY)
    dma = pltpu.SemaphoreType.DMA
    v = pltpu.VMEM
    gt, grads = pl.pallas_call(
        kernel,
        out_shape=(
            jax.ShapeDtypeStruct((TOK, D), BF16),
            jax.ShapeDtypeStruct((3 * F, DS), BF16),
        ),
        in_specs=[any_] * 7,
        out_specs=(any_,) * 2,
        scratch_shapes=[
            v((2, TOK), jnp.int32), v((2, TOK), F32),
            v((J, TOK, DS), BF16), v((J, TOK, DS), BF16),
            v((J, DS, 2 * F), BF16), v((J, F, DS), BF16),
            v((J, HALF, DS), BF16), v((HALF, DS), BF16),
            v((J, HALF, DS), BF16), v((HALF, DS), BF16),
            v((J, ROWS, DS), BF16), v((2 * HALF, DS), BF16),
            v((J, ROWS, DS), BF16), v((2 * HALF, DS), BF16),
            v((HALF, TOK), BF16), v((HALF, TOK), BF16),
            v((TOK, HALF), BF16), v((TOK, HALF), BF16),
            v((2, HALF, TOK), F32),
            v((ROWS, 2 * F), F32), v((ROWS, F), F32),
            v((ROWS, 2 * F), BF16), v((3 * F, ROWS), BF16),
            v((J, ROWS, DS), BF16), v((2 * HALF, DS), BF16),
            v((J, HALF, DS), BF16), v((HALF, DS), BF16),
            v((J, HALF, DS), BF16), v((HALF, DS), BF16),
            v((J, HALF, DS), BF16), v((HALF, DS), BF16),
            v((24, 4, UNIT, DS), BF16), v((12, UNIT, DS), BF16), v((16, UNIT, DS), F32),
            v((3 * F, DS), BF16),
            dma((8,)), dma((23,)), dma((23,)), dma((27,)), dma((27,)),
            dma((24, 4)), dma((24, 4)),
        ],
        compiler_params=pltpu.CompilerParams(
            collective_id=0, has_side_effects=True, vmem_limit_bytes=60 * 2**20
        ),
        cost_estimate=pl.CostEstimate(
            flops=15_000_000_000, bytes_accessed=14_000_000, transcendentals=500_000
        ),
    )(expert_ids.T, probs.T, tokens, cotangent, w_gate[0], w_up[0], w_down[0])
    gt, gg, gu, gd = pl.pallas_call(
        write_out,
        out_shape=(
            jax.ShapeDtypeStruct((TOK, D), BF16),
            jax.ShapeDtypeStruct((DS, F), BF16),
            jax.ShapeDtypeStruct((DS, F), BF16),
            jax.ShapeDtypeStruct((F, DS), BF16),
        ),
        in_specs=[any_] * 2,
        out_specs=(any_,) * 4,
        scratch_shapes=[v((TOK, D), BF16), v((3 * F, DS), BF16), v((2, DS, F), BF16), dma((14,))],
    )(gt, grads)
    return gt, gg[None], gu[None], gd[None]


def solution(mesh):
    in_specs = (
        P(("dp", "expert"), None),
        P(("dp", "expert"), None),
        P(("dp", "expert"), None),
        P(("dp", "expert"), None),
        P("expert", None, None),
        P("expert", None, None),
        P("expert", None, None),
    )
    out_specs = (
        P(("dp", "expert"), None),
        P("expert", "dp", None),
        P("expert", "dp", None),
        P("expert", None, "dp"),
    )
    return jax.shard_map(shards, mesh=mesh, in_specs=in_specs, out_specs=out_specs, check_vma=False)
```

```python
import jax
import jax.numpy as jnp
from jax import lax
from jax.experimental import pallas as pl
from jax.experimental.pallas import tpu as pltpu
from jax.sharding import PartitionSpec as P

D = 4096
F = 384
TOK = 128
N_DP = 8
CHIPS = 16
J = 8
DS = D // J
MAIN = 16
HALF = CHIPS * MAIN
ROWS = 2 * HALF + 64
UNIT = 96
MESH = pl.DeviceIdType.MESH
F32 = jnp.float32
BF16 = jnp.bfloat16
OTHERS = (
    (0, 1), (1, 0), (0, 3), (3, 0), (1, 1), (3, 3), (1, 3), (3, 1),
    (0, 2), (2, 0), (2, 1), (1, 2), (2, 3), (3, 2), (2, 2),
)
X_AT, XE_AT, S_AT, SE_AT, R_AT, RE_AT = 0, 8, 9, 17, 18, 22
RG_AT, RGE_AT = 18, 26
LAG = 3


def mm(a, b):
    return jnp.dot(a, b, preferred_element_type=F32)


def mm_nt(a, b):
    return lax.dot_general(a, b, (((1,), (1,)), ((), ())), preferred_element_type=F32)


def iota(shape, dim):
    return lax.broadcasted_iota(jnp.int32, shape, dim)


def eye(n):
    return (iota((n, n), 0) == iota((n, n), 1)).astype(BF16)


def kernel(
    ids_in, probs_in, tok, cot, wg, wu, wd,
    gt, grads,
    ids, probs, tokb, cotb, w_gu, w_d, xs, xse, ss, sse, X, XE, S, SE,
    pick, pick_e, pick_t, pick_et, scales, pre, gh, ggu, at,
    RG, RGE, RV, RVE, PS, PSE, RT, RTE, ring, begin, psum, gds,
    loc, snd, rcv, sib_s, sib_r, ring_s, ring_r,
):
    z = lax.axis_index("dp")
    e = lax.axis_index("expert")
    k = lax.rem(e, 2)
    c = e // 2
    cy = c // 4
    cx = lax.rem(c, 4)
    sibling = (z, c * 2 + (1 - k))
    z_next = (lax.rem(z + 1, N_DP), e)
    z_prev = (lax.rem(z + N_DP - 1, N_DP), e)
    chip_of = [lax.rem(cy + dy, 4) * 4 + lax.rem(cx + dx, 4) for dy, dx in OTHERS]

    barrier = pltpu.get_barrier_semaphore()
    for dev in (z_next, z_prev):
        pl.semaphore_signal(barrier, inc=1, device_id=dev, device_id_type=MESH)
    for chip in chip_of:
        pl.semaphore_signal(barrier, inc=1, device_id=(z, chip * 2 + k), device_id_type=MESH)
    pl.semaphore_signal(barrier, inc=1, device_id=sibling, device_id_type=MESH)
    pltpu.make_async_copy(ids_in, ids, loc.at[6]).start()
    pltpu.make_async_copy(probs_in, probs, loc.at[7]).start()
    for j in range(J):
        pltpu.make_async_copy(tok.at[:, pl.ds(j * DS, DS)], tokb.at[j], loc.at[0]).start()

    def wait_bytes(ref, sem):
        pltpu.make_async_copy(ref, ref, sem).wait()

    wait_bytes(ids, loc.at[6])
    wait_bytes(probs, loc.at[7])
    id0, id1 = ids[0:1, :], ids[1:2, :]
    p0, p1 = probs[0:1, :], probs[1:2, :]
    row = iota((HALF, TOK), 0)
    expert, slot = row // MAIN, lax.rem(row, MAIN)
    named0, named1 = id0 == expert, id1 == expert
    named = named0 | named1
    before = (iota((TOK, TOK), 0) < iota((TOK, TOK), 1)).astype(BF16)
    rank = mm(named.astype(F32).astype(BF16), before).astype(jnp.int32)
    main = named & (rank == slot)
    extra = named & (rank == MAIN + lax.rem(slot, 2))
    pick[...] = main.astype(F32).astype(BF16)
    pick_e[...] = extra.astype(F32).astype(BF16)

    def scale_of(picked):
        each = jnp.where(picked & named0, p0, 0.0) + jnp.where(picked & named1, p1, 0.0)
        return jnp.broadcast_to(jnp.sum(each, axis=1, keepdims=True), (HALF, TOK))

    scales[0] = scale_of(main)
    scales[1] = scale_of(extra)
    part = lax.rem(iota((HALF, TOK), 0), MAIN) // 2

    def extras_of(source):
        def add(j, total):
            chosen = jnp.where(part == j, pick_e[...].astype(F32), 0.0).astype(BF16)
            return total + mm(chosen, source[j])
        return lax.fori_loop(0, J, add, jnp.zeros((HALF, DS), F32))

    def blk(i):
        return pl.ds(pl.multiple_of(i * MAIN, MAIN), MAIN)

    def home(i):
        return pl.ds(pl.multiple_of(k * HALF + i * MAIN, MAIN), MAIN)

    mine = pl.ds(pl.multiple_of(k * HALF, HALF), HALF)
    theirs = pl.ds(pl.multiple_of((1 - k) * HALF, HALF), HALF)

    def send_all(src_of, dst, at_sem):
        for chip in chip_of:
            pltpu.make_async_remote_copy(
                src_ref=src_of(chip), dst_ref=dst,
                send_sem=snd.at[at_sem], recv_sem=rcv.at[at_sem],
                device_id=(z, chip * 2 + k), device_id_type=MESH,
            ).start()
        pltpu.make_async_copy(src_of(c), dst, rcv.at[at_sem]).start()

    def to_sibling(src, dst, at_sem):
        return pltpu.make_async_remote_copy(
            src_ref=src, dst_ref=dst, send_sem=sib_s.at[at_sem], recv_sem=sib_r.at[at_sem],
            device_id=sibling, device_id_type=MESH,
        )

    wait_bytes(tokb, loc.at[0])

    def send_tok(j):
        send_all(lambda i: xs.at[j, blk(i), :], X.at[j, home(c), :], X_AT + j)

    xs[0] = mm(pick[...], tokb[0]).astype(BF16)
    pl.semaphore_wait(barrier, len(OTHERS) + 3)
    send_tok(0)
    xse[...] = extras_of(tokb).astype(BF16)
    send_all(lambda i: xse.at[blk(i), :], XE.at[home(c), :], XE_AT)

    @pl.loop(1, J)
    def _(j):
        xs[j] = mm(pick[...], tokb[j]).astype(BF16)
        send_tok(j)

    for j in range(J):
        pltpu.make_async_copy(cot.at[:, pl.ds(j * DS, DS)], cotb.at[j], loc.at[1]).start()
    for j in range(J):
        rows = pl.ds(j * DS, DS)
        pltpu.make_async_copy(wg.at[rows, :], w_gu.at[j, :, pl.ds(0, F)], loc.at[2]).start()
        pltpu.make_async_copy(wu.at[rows, :], w_gu.at[j, :, pl.ds(F, F)], loc.at[2]).start()
    for j in range(J):
        pltpu.make_async_copy(wd.at[:, pl.ds(j * DS, DS)], w_d.at[j], loc.at[3]).start()

    wait_bytes(cotb, loc.at[1])
    sse[...] = (extras_of(cotb) * scales[1][:, 0:1]).astype(BF16)
    pick_t[...] = mm_nt(eye(TOK), pick[...]).astype(BF16)
    pick_et[...] = mm_nt(eye(TOK), pick_e[...]).astype(BF16)
    pre[...] = jnp.zeros_like(pre)
    gh[...] = jnp.zeros_like(gh)

    def place(t, up):
        return lax.rem(z + 12 - t, N_DP) if up else lax.rem(z + 4 + t, N_DP)

    def order(i):
        odd = lax.rem(i, 2)
        return place((i + 1) // 2, True) * odd + place(i // 2, False) * (1 - odd)

    def send_cot(i):
        o = order(i)
        ss[o] = (mm(pick[...], cotb[o]) * scales[0][:, 0:1]).astype(BF16)
        send_all(lambda n: ss.at[o, blk(n), :], S.at[o, home(c), :], S_AT + i)

    def unpack(j):
        r, col = iota((64, 2 * HALF), 0), iota((64, 2 * HALF), 1)
        return (col == (r // 2) * MAIN + 2 * j + lax.rem(r, 2)).astype(F32).astype(BF16)

    def unpack_t(j):
        r, col = iota((2 * HALF, 64), 1), iota((2 * HALF, 64), 0)
        return (col == (r // 2) * MAIN + 2 * j + lax.rem(r, 2)).astype(F32).astype(BF16)

    tail = pl.ds(2 * HALF, 64)

    wait_bytes(XE.at[pl.ds(0, HALF), :], rcv.at[XE_AT])
    fwd_xe = to_sibling(XE.at[mine, :], XE.at[mine, :], XE_AT)
    fwd_xe.start()
    fwd_xe.wait_recv()

    @pl.loop(0, J)
    def _(j):
        X[j, tail, :] = mm(unpack(j), XE[...]).astype(BF16)

    send_all(lambda i: sse.at[blk(i), :], SE.at[home(c), :], SE_AT)
    wait_bytes(w_gu, loc.at[2])

    @pl.loop(0, J)
    def _(j):
        wait_bytes(X.at[j, pl.ds(0, HALF), :], rcv.at[X_AT + j])
        fwd = to_sibling(X.at[j, mine, :], X.at[j, mine, :], X_AT + j)
        fwd.start()

        @pl.when(j >= LAG)
        def _():
            send_cot(j - LAG)

        fwd.wait_recv()
        pre[...] += mm(X[j], w_gu[j])

    def store_t(first, value):
        at[pl.ds(first, F), :] = mm_nt(eye(F), value).astype(BF16)

    gate, up = pre[:, 0:F], pre[:, F:2 * F]
    store_t(2 * F, (gate * jax.nn.sigmoid(gate) * up).astype(BF16))

    def several(first, last, what):
        @pl.loop(first, last)
        def _(n):
            what(n)

    def pass_on(v, t, src, up):
        pltpu.make_async_remote_copy(
            src_ref=src, dst_ref=ring.at[v, t],
            send_sem=ring_s.at[v, t], recv_sem=ring_r.at[v, t],
            device_id=z_next if up else z_prev, device_id_type=MESH,
        ).start()

    down, gate_up = (0, 4, 2 * F, 3), (4, 8, 0, 3)

    def begin_chains(group, source):
        u0, n, first, lo = group
        terms = mm(at[pl.ds(first, n * UNIT), :], source[place(0, False)])
        for m in range(n):
            begin[u0 + m] = terms[m * UNIT:(m + 1) * UNIT].astype(BF16)

        @pl.loop(0, lo)
        def _(m):
            pass_on(u0 + m, 0, begin.at[u0 + m], False)

        @pl.loop(lo, n)
        def _(m):
            pass_on(12 + u0 + m, 0, begin.at[u0 + m], True)

    def terms_of(group, t, up, source):
        u0, n, first, lo = group
        terms = mm(at[pl.ds(first, n * UNIT), :], source[place(t, up)])
        for m in range(n):
            psum[up * 8 + m] = terms[m * UNIT:(m + 1) * UNIT]

    def hop(group, m, t, up, joins):
        v = up * 12 + group[0] + m
        slot_ref = ring.at[v, t - 1]
        if joins:
            wait_bytes(slot_ref, ring_r.at[v, t - 1])
            slot_ref[...] = (psum[up * 8 + m] + slot_ref[...].astype(F32)).astype(BF16)
        else:
            slot_ref[...] = psum[up * 8 + m].astype(BF16)
        pass_on(v, t, slot_ref, up)

    def hops(group, t, half, ups):
        _, n, _, lo = group
        places = (half * n // 2, (half + 1) * n // 2)
        if t == 1:
            for i in range(*places):
                for up in ups:
                    m = i if up else (i + lo) % n
                    hop(group, m, t, up, (m >= lo) == bool(up))
            return

        @pl.loop(*places)
        def _(i):
            for up in ups:
                hop(group, i if up else lax.rem(i + lo, n), t, up, True)

    def end_chains(group, source):
        u0, n, first, lo = group
        terms_of(group, 4, 0, source)

        def end(m):
            for up in range(2):
                wait_bytes(ring.at[up * 12 + u0 + m, 3], ring_r.at[up * 12 + u0 + m, 3])
            came = ring[u0 + m, 3].astype(F32) + ring[12 + u0 + m, 3].astype(F32)
            rows = pl.ds(pl.multiple_of(first + m * UNIT, UNIT), UNIT)
            gds[rows, :] = (psum[m] + came).astype(BF16)

        if n < 2 * lo:
            several(0, n, end)
            return
        several(lo, n - lo, end)

        @pl.loop(0, lo)
        def _(m):
            end(m)
            end(n - lo + m)

    def forward(i):
        o = order(i)
        wait_bytes(S.at[o, pl.ds(0, HALF), :], rcv.at[S_AT + i])
        to_sibling(S.at[o, mine, :], S.at[o, mine, :], S_AT + i).start()

    def fill_tail(i):
        o = order(i)
        S[o, tail, :] = mm(unpack(o), SE[...]).astype(BF16)

    def here(i):
        o = order(i)
        to_sibling(S.at[o, mine, :], S.at[o, mine, :], S_AT + i).wait_recv()

    def grad_hidden(i):
        o = order(i)
        gh[...] += mm_nt(S[o], w_d[o])

    def down_step(t, up):
        terms_of(down, t, up, S)
        hops(down, t, 0, (up,))
        hops(down, t, 1, (up,))

    wait_bytes(SE.at[pl.ds(0, HALF), :], rcv.at[SE_AT])
    fwd_se = to_sibling(SE.at[mine, :], SE.at[mine, :], SE_AT)
    fwd_se.start()
    forward(0)
    fwd_se.wait_recv()
    fill_tail(0)
    here(0)
    begin_chains(down, S)

    wait_bytes(w_d, loc.at[3])
    for i in range(1, 7):
        forward(i)
        if i <= LAG:
            send_cot(J - LAG + i - 1)
        fill_tail(i)
        grad_hidden(i - 1)
        here(i)
        if i == 6:
            forward(7)
            fill_tail(7)
        down_step((i + 1) // 2, i % 2)
    grad_hidden(6)
    here(7)
    grad_hidden(7)

    gate, up, grad = pre[:, 0:F], pre[:, F:2 * F], gh[...]
    sig = jax.nn.sigmoid(gate)
    ggate = (grad * up * sig * (1.0 + gate * (1.0 - sig))).astype(BF16)
    gup = (grad * gate * sig).astype(BF16)
    ggu[:, 0:F] = ggate
    ggu[:, F:2 * F] = gup
    store_t(0, ggate)
    store_t(F, gup)

    def row_grad(j):
        RG[j] = mm_nt(ggu[...], w_gu[j]).astype(BF16)
        to_sibling(RG.at[j, theirs, :], RV.at[j], RG_AT + j).start()

    def pair_grad(q):
        for n in range(2):
            j = 2 * q + n
            to_sibling(RG.at[j, theirs, :], RV.at[j], RG_AT + j).wait_recv()
            PS[j] = (RG[j, mine, :].astype(F32) + RV[j].astype(F32)).astype(BF16)
        two = pl.ds(2 * q, 2)
        send_all(lambda i: PS.at[two, blk(i), :], RT.at[two, blk(c), :], R_AT + q)

    def row_grad_extras():
        def add(j, total):
            return total + mm(unpack_t(j), RG[j, tail, :])
        RGE[...] = lax.fori_loop(0, J, add, jnp.zeros((2 * HALF, DS), F32)).astype(BF16)
        to_sibling(RGE.at[theirs, :], RVE, RGE_AT).start()

    def pair_grad_extras():
        to_sibling(RGE.at[theirs, :], RVE, RGE_AT).wait_recv()
        PSE[...] = (RGE[mine, :].astype(F32) + RVE[...].astype(F32)).astype(BF16)
        send_all(lambda i: PSE.at[blk(i), :], RTE.at[blk(c), :], RE_AT)

    part_col = lax.rem(iota((TOK, HALF), 1), MAIN) // 2

    def token_grad(q):
        two = pl.ds(2 * q, 2)
        wait_bytes(RT.at[two], rcv.at[R_AT + q])
        for n in range(2):
            j = 2 * q + n
            chosen = jnp.where(part_col == j, pick_et[...].astype(F32), 0.0).astype(BF16)
            tokb[j] = (mm(pick_t[...], RT[j]) + mm(chosen, RTE[...])).astype(BF16)
            cols = pl.ds(pl.multiple_of(j * DS, DS), DS)
            pltpu.make_async_copy(tokb.at[j], gt.at[:, cols], loc.at[4]).start()

    begin_chains(gate_up, X)
    several(0, 4, row_grad)
    for t in range(1, 4):
        terms_of(gate_up, t, 1, X)
        terms_of(gate_up, t, 0, X)
        hops(gate_up, t, 0, (1, 0))
        if t == 1:
            several(4, 8, row_grad)
            pair_grad(0)
            pair_grad(1)
        if t == 2:
            pair_grad_extras()
        hops(gate_up, t, 1, (1, 0))
        if t == 1:
            several(2, 4, pair_grad)
            row_grad_extras()
    end_chains(down, S)
    def out(first, rows):
        rows = pl.ds(first, rows)
        pltpu.make_async_copy(gds.at[rows, :], grads.at[rows, :], loc.at[5]).start()

    out(2 * F, F)
    wait_bytes(RTE, rcv.at[RE_AT])
    several(0, 4, token_grad)

    def sent(ref, sem):
        wait_bytes(ref, sem)

    less = HALF - MAIN
    for q in range(4):
        two = pl.ds(2 * q, 2)
        sent(PS.at[two, pl.ds(0, less), :], snd.at[R_AT + q])
    for i in range(J):
        sent(xs.at[i, pl.ds(0, less), :], snd.at[X_AT + i])
        sent(ss.at[i, pl.ds(0, less), :], snd.at[S_AT + i])
        sent(xs.at[i], sib_s.at[X_AT + i])
        sent(ss.at[i], sib_s.at[S_AT + i])
        sent(RV.at[i], sib_s.at[RG_AT + i])
    for at_sem in (XE_AT, SE_AT, RE_AT):
        sent(xse.at[pl.ds(0, less), :], snd.at[at_sem])
    for at_sem in (XE_AT, SE_AT, RGE_AT):
        sent(xse, sib_s.at[at_sem])

    for u0, n, _, lo in (down, gate_up):
        for m in range(n):
            sent(begin.at[0], ring_s.at[u0 + m + (0 if m < lo else 12), 0])

    @pl.loop(0, 24)
    def _(v):
        for t in range(1, 3):
            sent(ring.at[v, t], ring_s.at[v, t])

    wait_bytes(tokb, loc.at[4])
    end_chains(gate_up, X)
    out(0, 2 * F)

    @pl.loop(0, 24)
    def _(v):
        sent(ring.at[v, 3], ring_s.at[v, 3])

    wait_bytes(gds, loc.at[5])


def write_out(gt, grads, gt_out, gg_out, gu_out, gd_out, gt_v, grads_v, turned, sem):
    parts = [
        pltpu.make_async_copy(grads.at[pl.ds(n * F, F), :], grads_v.at[pl.ds(n * F, F), :], sem.at[n])
        for n in range(3)
    ]
    rows = [pl.ds(32 * n, 32) for n in range(4)]
    tokens = [pltpu.make_async_copy(gt.at[r, :], gt_v.at[r, :], sem.at[3 + n]) for n, r in enumerate(rows)]
    for read in tokens + parts[::-1]:
        read.start()
    writes = []

    def write(src, dst):
        writes.append(pltpu.make_async_copy(src, dst, sem.at[7 + len(writes)]))
        writes[-1].start()

    for n, r in enumerate(rows):
        tokens[n].wait()
        write(gt_v.at[r, :], gt_out.at[r, :])
    parts[2].wait()
    write(grads_v.at[pl.ds(2 * F, F), :], gd_out)
    for n, dst in enumerate((gg_out, gu_out)):
        parts[n].wait()
        turned[n] = mm_nt(eye(DS), grads_v[n * F:(n + 1) * F, :]).astype(BF16)
        write(turned.at[n], dst)
    for copy in writes:
        copy.wait()


def shards(tokens, cotangent, expert_ids, probs, w_gate, w_up, w_down):
    any_ = pl.BlockSpec(memory_space=pl.ANY)
    dma = pltpu.SemaphoreType.DMA
    v = pltpu.VMEM
    gt, grads = pl.pallas_call(
        kernel,
        out_shape=(
            jax.ShapeDtypeStruct((TOK, D), BF16),
            jax.ShapeDtypeStruct((3 * F, DS), BF16),
        ),
        in_specs=[any_] * 7,
        out_specs=(any_,) * 2,
        scratch_shapes=[
            v((2, TOK), jnp.int32), v((2, TOK), F32),
            v((J, TOK, DS), BF16), v((J, TOK, DS), BF16),
            v((J, DS, 2 * F), BF16), v((J, F, DS), BF16),
            v((J, HALF, DS), BF16), v((HALF, DS), BF16),
            v((J, HALF, DS), BF16), v((HALF, DS), BF16),
            v((J, ROWS, DS), BF16), v((2 * HALF, DS), BF16),
            v((J, ROWS, DS), BF16), v((2 * HALF, DS), BF16),
            v((HALF, TOK), BF16), v((HALF, TOK), BF16),
            v((TOK, HALF), BF16), v((TOK, HALF), BF16),
            v((2, HALF, TOK), F32),
            v((ROWS, 2 * F), F32), v((ROWS, F), F32),
            v((ROWS, 2 * F), BF16), v((3 * F, ROWS), BF16),
            v((J, ROWS, DS), BF16), v((2 * HALF, DS), BF16),
            v((J, HALF, DS), BF16), v((HALF, DS), BF16),
            v((J, HALF, DS), BF16), v((HALF, DS), BF16),
            v((J, HALF, DS), BF16), v((HALF, DS), BF16),
            v((24, 4, UNIT, DS), BF16), v((12, UNIT, DS), BF16), v((16, UNIT, DS), F32),
            v((3 * F, DS), BF16),
            dma((8,)), dma((23,)), dma((23,)), dma((27,)), dma((27,)),
            dma((24, 4)), dma((24, 4)),
        ],
        compiler_params=pltpu.CompilerParams(
            collective_id=0, has_side_effects=True, vmem_limit_bytes=60 * 2**20
        ),
        cost_estimate=pl.CostEstimate(
            flops=15_000_000_000, bytes_accessed=14_000_000, transcendentals=500_000
        ),
    )(expert_ids.T, probs.T, tokens, cotangent, w_gate[0], w_up[0], w_down[0])
    gt, gg, gu, gd = pl.pallas_call(
        write_out,
        out_shape=(
            jax.ShapeDtypeStruct((TOK, D), BF16),
            jax.ShapeDtypeStruct((DS, F), BF16),
            jax.ShapeDtypeStruct((DS, F), BF16),
            jax.ShapeDtypeStruct((F, DS), BF16),
        ),
        in_specs=[any_] * 2,
        out_specs=(any_,) * 4,
        scratch_shapes=[v((TOK, D), BF16), v((3 * F, DS), BF16), v((2, DS, F), BF16), dma((14,))],
    )(gt, grads)
    return gt, gg[None], gu[None], gd[None]


def solution(mesh):
    in_specs = (
        P(("dp", "expert"), None),
        P(("dp", "expert"), None),
        P(("dp", "expert"), None),
        P(("dp", "expert"), None),
        P("expert", None, None),
        P("expert", None, None),
        P("expert", None, None),
    )
    out_specs = (
        P(("dp", "expert"), None),
        P("expert", "dp", None),
        P("expert", "dp", None),
        P("expert", None, "dp"),
    )
    return jax.shard_map(shards, mesh=mesh, in_specs=in_specs, out_specs=out_specs, check_vma=False)
```
